256 devices in a mesh: blk: 64 (over z, x, core), grp: 4 (over y).
Axes of the slice: x: 4, y: 4, z: 8, core: 2. Of those that a mesh axis runs over, the one named last changes fastest.
Arguments:
- features: bfloat16 [131072, 128], P(('blk', 'grp')), may hold values from -6 to 6
- weight: bfloat16 [128, 256], replicated, may hold values from -0.5 to 0.5
- cotangent: bfloat16 [131072, 256], P(('blk', 'grp')), may hold values from -6 to 6
- tiles: bfloat16 [16384, 128, 128], P(('blk', 'grp')), may hold values from -0.125 to 0.125
- tile_row: int32 [16384], P(('blk', 'grp')), may hold values from 0 to 3
- tile_col: int32 [16384], P(('blk', 'grp')), may hold values from 0 to 23
- hub_index: int32 [32768], P(('blk', 'grp')), may hold values from 0 to 511
- send_index: int32 [16384, 32], P(('blk', 'grp')), may hold values from 0 to 511
- send_count: int32 [16384], P(('blk', 'grp')), may hold values from 1 to 32, as said below
Outputs:
- activations: bfloat16 [131072, 256], P(('blk', 'grp'))
- weight_grad: float32 [128, 256], replicated
- feature_grad: float32 [131072, 128], P(('blk', 'grp'))
The draws below stay inside these ranges and needn't reach their ends.
Inputs may be any that keep to these rules, and one draw needn't show every extreme that they name: `send_count`: each device has at least one destination whose count is 32.
All inputs are finite; a program needn't handle non-finite values.
Results may differ from the reference program's by a relative error of at most 0.0085.
Values may be sent and summed in bfloat16 or wider, within the bound.
A program may use at most 64 MiB of HBM per device.

```python
import jax
import jax.numpy as jnp
from jax import lax

FIN = 128
FOUT = 256
TILE = 128
R = 512
TPR = 16
SLOT = 32
HUB_DEV = 128
NODES = 131072
TILES = 64
ROW_TILES = 4
SRC_TILES = 24
N_BLK = 64
N_GRP = 4
DEVICES = 256


def draw_send_count(key, part):
    key = jax.random.fold_in(key, 11)
    first_key, second_key = jax.random.split(key)
    counts = jax.random.randint(first_key, (DEVICES, N_BLK), 1, SLOT + 1)
    chosen = jax.random.randint(second_key, (DEVICES, 1), 0, N_BLK)
    column = lax.broadcasted_iota(jnp.int32, (DEVICES, N_BLK), 1)
    return jnp.where(column == chosen, SLOT, counts).reshape(DEVICES * N_BLK).astype(jnp.int32)


def touch_ends(result, key, smallest, high):
    spot = [jax.random.randint(jax.random.fold_in(key, axis), (), 0, length) for axis, length in enumerate(result.shape)]
    widest = result.shape.index(max(result.shape))
    beside = spot[:widest] + [(spot[widest] + 1) % result.shape[widest]] + spot[widest + 1:]
    return result.at[tuple(spot)].set(smallest).at[tuple(beside)].set(high)


def shard_levels(key, dims, cuts, smallest, high):
    def one(position, shards_of):
        heights = jax.random.uniform(jax.random.fold_in(jax.random.fold_in(key, 6), position), (shards_of,), jnp.float32, smallest / len(cuts), high / len(cuts))
        return jnp.repeat(jnp.exp(heights), dims[position] // shards_of).reshape((-1,) + (1,) * (len(dims) - position - 1))

    factor_of = one(*cuts[0])
    for cut in cuts[1:]:
        factor_of = factor_of * one(*cut)
    return factor_of


def normal_values(own_key, shape, deviation, most, cuts=(), held_as=jnp.bfloat16):
    level = shard_levels(own_key, shape, cuts, -0.22, 0.18) if cuts else 1.0
    values = jax.random.normal(own_key, shape, jnp.float32) * deviation * level
    return jnp.minimum(jnp.maximum(values, -most), most).astype(held_as)


def setup_inputs(seed: int = 0) -> dict:
    arg_keys = jax.random.split(jax.random.key(seed), 10)
    return {
        "features": normal_values(arg_keys[0], (NODES, FIN), 1.0, 6.0, ((0, 256),)),
        "weight": normal_values(arg_keys[1], (FIN, FOUT), FIN ** -0.5, 0.5),
        "cotangent": normal_values(arg_keys[2], (NODES, FOUT), 1.0, 6.0, ((0, 256),)),
        "tiles": normal_values(arg_keys[3], (DEVICES * TILES, TILE, TILE), (TPR * TILE) ** -0.5, 0.125, ((0, 256),)),
        "tile_row": touch_ends(jax.random.randint(arg_keys[4], (DEVICES * TILES,), 0, ROW_TILES), jax.random.fold_in(arg_keys[4], 1), 0, ROW_TILES - 1).astype(jnp.int32),
        "tile_col": touch_ends(jax.random.randint(arg_keys[5], (DEVICES * TILES,), 0, SRC_TILES), jax.random.fold_in(arg_keys[5], 1), 0, SRC_TILES - 1).astype(jnp.int32),
        "hub_index": touch_ends(jax.random.randint(arg_keys[6], (DEVICES * HUB_DEV,), 0, R), jax.random.fold_in(arg_keys[6], 1), 0, R - 1).astype(jnp.int32),
        "send_index": touch_ends(jax.random.randint(arg_keys[7], (DEVICES * N_BLK, SLOT), 0, R), jax.random.fold_in(arg_keys[7], 1), 0, R - 1).astype(jnp.int32),
        "send_count": draw_send_count(jax.random.fold_in(arg_keys[9], 71), 0),
    }


def silu_grad(values):
    logistic = jax.nn.sigmoid(values)
    return logistic * (1.0 + values * (1.0 - logistic))

def take_rows(node_rows, picks):
    return node_rows[picks]

def reference(features, weight, cotangent, tiles, tile_row, tile_col, hub_index, send_index, send_count):
    device_count = N_BLK * N_GRP
    width_in = features.shape[1]
    width_out = weight.shape[1]
    node_rows = features.reshape(N_BLK, N_GRP, R, width_in)
    send_rows = send_index.reshape(N_BLK, N_GRP, N_BLK, SLOT)
    counts = send_count.reshape(N_BLK, N_GRP, N_BLK)
    slot_live = jnp.arange(SLOT, dtype=jnp.int32)[None, None, None, :] < counts[..., None]
    outgoing = jax.vmap(jax.vmap(take_rows))(node_rows, send_rows.reshape(N_BLK, N_GRP, N_BLK * SLOT))
    outgoing = outgoing.reshape(N_BLK, N_GRP, N_BLK, SLOT, width_in)
    outgoing = jnp.where(slot_live[..., None], outgoing, jnp.zeros((), outgoing.dtype))
    incoming = jnp.transpose(outgoing, (2, 1, 0, 3, 4)).reshape(N_BLK, N_GRP, N_BLK * SLOT, width_in)
    hub_table = jax.vmap(jax.vmap(take_rows))(node_rows, hub_index.reshape(N_BLK, N_GRP, HUB_DEV))
    hub_table = jnp.broadcast_to(hub_table.reshape(N_BLK, 1, N_GRP * HUB_DEV, width_in), (N_BLK, N_GRP, N_GRP * HUB_DEV, width_in))
    sources = jnp.concatenate([node_rows, incoming, hub_table], axis=2).reshape(device_count, SRC_TILES, TILE, width_in)
    tile_sets = tiles.reshape(device_count, TILES, TILE, TILE)
    row_index = tile_row.reshape(device_count, TILES)
    column_index = tile_col.reshape(device_count, TILES)

    def forward(pieces):
        source_set, tile_set, row_set, column_set = pieces
        products = jnp.einsum('lij,ljf->lif', tile_set.astype(jnp.float32), source_set[column_set].astype(jnp.float32))
        summed = jax.ops.segment_sum(products, row_set, num_segments=ROW_TILES)
        return summed.reshape(R, width_in).astype(jnp.bfloat16)
    aggregated = lax.map(forward, (sources, tile_sets, row_index, column_index)).reshape(NODES, width_in)
    preact = jnp.dot(aggregated, weight, preferred_element_type=jnp.float32)
    activations = jax.nn.silu(preact).astype(jnp.bfloat16)
    pre_grad = (cotangent.astype(jnp.float32) * silu_grad(preact)).astype(jnp.bfloat16)
    weight_grad = jnp.dot(aggregated.T, pre_grad, preferred_element_type=jnp.float32)
    transposed = weight.astype(jnp.float32).T
    grad_tiles = pre_grad.reshape(device_count, ROW_TILES, TILE, width_out)

    def backward(pieces):
        grad_set, tile_set, row_set, column_set = pieces
        products = jnp.einsum('lij,lif->ljf', tile_set.astype(jnp.float32), grad_set[row_set].astype(jnp.float32))
        summed = jax.ops.segment_sum(products, column_set, num_segments=SRC_TILES).reshape(SRC_TILES * TILE, width_out)
        return jnp.dot(summed, transposed, precision=lax.Precision.HIGHEST)
    narrow_grad = lax.map(backward, (grad_tiles, tile_sets, row_index, column_index)).reshape(N_BLK, N_GRP, SRC_TILES * TILE, width_in)
    own_part = narrow_grad[:, :, :R]
    boundary = narrow_grad[:, :, R:R + N_BLK * SLOT].reshape(N_BLK, N_GRP, N_BLK, SLOT, width_in)
    returned = jnp.transpose(boundary, (2, 1, 0, 3, 4))
    returned = jnp.where(slot_live[..., None], returned, jnp.zeros((), returned.dtype))
    hub_grad = narrow_grad[:, :, R + N_BLK * SLOT:].reshape(N_BLK, N_GRP, N_GRP, HUB_DEV, width_in).sum(axis=1)
    offsets = (jnp.arange(device_count, dtype=jnp.int32) * R).reshape(N_BLK, N_GRP)
    boundary_at = (offsets[:, :, None, None] + send_rows).astype(jnp.int32)
    hub_at = (offsets[:, :, None] + hub_index.reshape(N_BLK, N_GRP, HUB_DEV)).astype(jnp.int32)
    feature_grad = own_part.reshape(NODES, width_in)
    feature_grad = feature_grad.at[boundary_at.reshape(-1)].add(returned.reshape(-1, width_in))
    feature_grad = feature_grad.at[hub_at.reshape(-1)].add(hub_grad.reshape(-1, width_in))
    return (activations, weight_grad, feature_grad)
```

```python
import functools

import jax
import jax.numpy as jnp
from jax import lax
from jax.experimental import pallas as pl
from jax.experimental.pallas import tpu as pltpu
from jax.sharding import PartitionSpec as P

TILE = 128
MESH = pl.DeviceIdType.MESH
BF16 = jnp.bfloat16
F32 = jnp.float32


def dot(left, right):
    return lax.dot_general(left, right, (((1,), (0,)), ((), ())), preferred_element_type=F32)


def dot_t(left, right):
    return lax.dot_general(left, right, (((0,), (0,)), ((), ())), preferred_element_type=F32)


def iota(shape, axis):
    return lax.broadcasted_iota(jnp.int32, shape, axis)


def kernel(
    nb, ng, inner,
    feat_h, w_h, wt_h, cot_h, tiles_h, trow_h, tcol_h, hub_h, sidx_h, scnt_h,
    act_h, wg_h, fg_h,
    feat, w, wt, cot, tiles, trow, tcol, hub, sidx, scnt,
    cntm, idxm, sendbuf, incoming, hubs, hubsend, ohT, ohhubT,
    info, info_s, run, runT, A, AT, agg, aggb, pg, gb, act, retbuf, ret, hubret_send, hubret,
    part, ybuf, q3, xbuf, zbuf, zown, f3, wbuf, wg, own,
    in_sems, s1, r1, sh1, rh1, s2, r2, sh2, rh2, ar_s, ar_r, loc_sem, out_sems,
):
    rows = feat.shape[0]
    row_tiles = rows // TILE
    slots = sidx.shape[1]
    per_chunk = TILE // slots
    chunks = nb // per_chunk
    tile_count = tiles.shape[0]
    nz = nb // inner
    halves = inner // per_chunk
    src_tiles = row_tiles + chunks + ng
    b = lax.axis_index("blk")
    g = lax.axis_index("grp")
    z = b // inner
    ii = lax.rem(b, inner)
    half = ii // per_chunk
    lane_dev = lax.rem(b, per_chunk)

    ins = [
        (sidx_h, sidx.at[pl.ds(0, nb)]), (scnt_h, scnt), (feat_h, feat), (hub_h, hub), (trow_h, trow),
        (tcol_h, tcol), (tiles_h, tiles), (w_h, w), (wt_h, wt), (cot_h, cot),
    ]
    loads = [pltpu.make_async_copy(h, v, in_sems.at[i]) for i, (h, v) in enumerate(ins)]
    for load in loads:
        load.start()

    barrier = pltpu.get_barrier_semaphore()

    def greet_blk(k, _):
        pl.semaphore_signal(barrier, inc=1, device_id=(lax.rem(b + k, nb), g), device_id_type=MESH)
        return 0

    def greet_grp(k, _):
        pl.semaphore_signal(barrier, inc=1, device_id=(b, lax.rem(g + k, ng)), device_id_type=MESH)
        return 0

    lax.fori_loop(1, nb, greet_blk, 0)
    lax.fori_loop(1, ng, greet_grp, 0)

    loads[0].wait()
    loads[1].wait()
    lane1 = iota((1, TILE), 1)
    for i in range(chunks):
        row = jnp.full((1, TILE), scnt[i * per_chunk], jnp.int32)
        for q in range(1, per_chunk):
            row = jnp.where(lane1 >= q * slots, scnt[i * per_chunk + q], row)
        cntm[i:i + 1, :] = row
    idx = jnp.concatenate(
        [sidx[pl.ds(q, chunks, stride=per_chunk), :] for q in range(per_chunk)], axis=1
    )
    slot_of = lax.rem(iota((chunks, TILE), 1), slots)
    idxm[0:chunks, :] = jnp.where(slot_of < cntm[0:chunks, :], idx, -1).astype(F32)
    loads[3].wait()
    idxm[chunks:chunks + 1, :] = hub[...].astype(F32)
    loads[2].wait()

    pl.semaphore_wait(barrier, nb - 1 + ng - 1)

    lane_rows = iota((TILE, rows), 1).astype(F32)

    def gather(row):
        column = jnp.transpose(jnp.broadcast_to(row, (TILE, TILE)))
        wide = jnp.concatenate([column] * row_tiles, axis=1)
        onehot = jnp.where(wide == lane_rows, 1.0, 0.0).astype(BF16)
        return dot(onehot, feat[...]).astype(BF16)

    def chunk_at(j):
        m = j // halves
        e = lax.rem(j, halves)
        step = (m + 1) // 2
        dz = jnp.where(lax.rem(m, 2) == 1, nz // 2 - step, nz - nz // 2 + step)
        return lax.rem(z + dz, nz) * halves + lax.rem(half + e, halves)

    def exchange(buffer, landing, ssem, rsem, j, ci):
        for q in range(per_chunk):
            piece = lax.rem(lane_dev + q, per_chunk)
            source = buffer.at[j, pl.ds(pl.multiple_of(piece * slots, slots), slots)]
            target = landing.at[pl.ds(pl.multiple_of(b * slots, slots), slots)]
            to = ci * per_chunk + piece

            def send(source=source, target=target, to=to):
                pltpu.make_async_remote_copy(
                    src_ref=source, dst_ref=target, send_sem=ssem, recv_sem=rsem,
                    device_id=(to, g), device_id_type=MESH,
                ).start()

            if q == 0:
                @pl.when(to != b)
                def _():
                    send()

                @pl.when(to == b)
                def _():
                    pltpu.make_async_copy(source, target, rsem).start()
            else:
                send()

    hubsend[...] = gather(idxm[chunks:chunks + 1, :])
    hubs[g] = hubsend[...]
    for k in range(1, ng):
        pltpu.make_async_remote_copy(
            src_ref=hubsend, dst_ref=hubs.at[g], send_sem=sh1, recv_sem=rh1,
            device_id=(b, lax.rem(g + k, ng)), device_id_type=MESH,
        ).start()

    def send_chunk(j, _):
        ci = chunk_at(j)
        sendbuf[j] = gather(idxm[pl.ds(ci, 1), :])
        exchange(sendbuf, incoming, s1, r1, j, ci)
        return 0

    lax.fori_loop(0, chunks, send_chunk, 0)

    loads[4].wait()
    loads[5].wait()
    cells = row_tiles * src_tiles
    pad = jnp.full((1, TILE - tile_count), cells + 4, jnp.int32)
    key = jnp.concatenate([trow[...] * src_tiles + tcol[...], pad], axis=1) if tile_count < TILE else trow[...] * src_tiles + tcol[...]
    full = (TILE, TILE)
    lane = iota(full, 1)
    sub = iota(full, 0)

    def count(mask, values=1):
        return jnp.sum(jnp.where(mask, values, 0), axis=0, keepdims=True)

    key_l = jnp.broadcast_to(key, full)
    key_s = jnp.transpose(key_l)
    before = jnp.logical_or(key_s < key_l, jnp.logical_and(key_s == key_l, sub < lane))
    rank_s = jnp.transpose(jnp.broadcast_to(count(before), full))
    sorted_key = count(rank_s == lane, key_s)
    former_key = count(rank_s == lane - 1, key_s)
    first = jnp.where(jnp.logical_or(sorted_key != former_key, lane[0:1] == 0), 1, 0)
    upto = count(key_s <= lane)
    last = jnp.where(count(key_s == lane) > 0, upto - 1, tile_count)
    info[0:1, :] = jnp.clip(count(rank_s == lane, sub), 0, tile_count - 1)
    info[1:2, :] = first
    info[2:3, :] = jnp.clip(last, 0, tile_count)
    info[3:8, :] = jnp.zeros((5, TILE), jnp.int32)
    to_scalars = pltpu.make_async_copy(info, info_s, loc_sem)
    to_scalars.start()
    to_scalars.wait()

    loads[6].wait()
    run[tile_count] = jnp.zeros(full, BF16)
    runT[tile_count] = jnp.zeros(full, BF16)

    def add_tile(k, total):
        value = tiles[jnp.clip(info_s[0, k], 0, tile_count - 1)].astype(F32)
        total = jnp.where(info_s[1, k] == 1, value, total + value)
        run[k] = total.astype(BF16)
        runT[k] = jnp.transpose(total).astype(BF16)
        return total

    lax.fori_loop(0, tile_count, add_tile, jnp.zeros(full, F32))

    def place(c, _):
        at = pl.ds(pl.multiple_of(c * TILE, TILE), TILE)
        for r in range(row_tiles):
            cell = jnp.clip(info_s[2, r * src_tiles + c], 0, tile_count)
            A[r * TILE:(r + 1) * TILE, at] = run[cell]
            AT[c, :, r * TILE:(r + 1) * TILE] = runT[cell]
        return 0

    lax.fori_loop(0, src_tiles, place, 0)

    sub_rows = iota((rows, TILE), 0).astype(F32)

    def columns(i, _):
        row = idxm[pl.ds(i, 1), :]
        ohT[:, pl.ds(pl.multiple_of(i * TILE, TILE), TILE)] = jnp.where(sub_rows == row, 1.0, 0.0).astype(BF16)
        return 0

    lax.fori_loop(0, chunks, columns, 0)
    ohhubT[...] = jnp.where(sub_rows == idxm[chunks:chunks + 1, :], 1.0, 0.0).astype(BF16)

    lo, hi = rows, rows + chunks * TILE
    pltpu.make_async_copy(hubs.at[pl.ds(0, ng - 1)], hubs.at[pl.ds(0, ng - 1)], rh1).wait()
    agg[...] = dot(A[:, 0:lo], feat[...]) + dot(A[:, hi:], hubs[...].reshape(ng * TILE, TILE))
    for i in range(7, 10):
        loads[i].wait()
    pltpu.make_async_copy(incoming, incoming, r1).wait()
    for r in range(row_tiles):
        at = slice(r * TILE, (r + 1) * TILE)
        summed = (agg[at, :] + dot(A[at, lo:hi], incoming[...])).astype(BF16)
        aggb[at, :] = summed
        preact = dot(summed, w[...])
        logistic = 1.0 / (1.0 + jnp.exp(-preact))
        act[at, :] = (preact * logistic).astype(BF16)
        grad = (cot[at, :].astype(F32) * (logistic * (1.0 + preact * (1.0 - logistic)))).astype(BF16)
        pg[at, :] = grad
        gb[at, :] = dot(grad, wt[...]).astype(BF16)
    act_out = pltpu.make_async_copy(act, act_h, out_sems.at[0])
    act_out.start()

    part[...] = dot_t(aggb[...], pg[...])
    q_rows = TILE // ng

    def q_of(k):
        return part.at[pl.ds(pl.multiple_of(k * q_rows, q_rows), q_rows)]

    for k in range(1, ng):
        to = lax.rem(g + k, ng)
        pltpu.make_async_remote_copy(
            src_ref=q_of(to), dst_ref=ybuf.at[ng - 1 - k], send_sem=ar_s.at[0], recv_sem=ar_r.at[0],
            device_id=(b, to), device_id_type=MESH,
        ).start()

    def back_chunk(j, _):
        ci = chunk_at(j)
        retbuf[j] = dot(AT[row_tiles + ci], gb[...]).astype(BF16)
        exchange(retbuf, ret, s2, r2, j, ci)
        return 0

    lax.fori_loop(0, chunks, back_chunk, 0)
    for k in range(ng):
        hubret_send[k] = dot(AT[row_tiles + chunks + k], gb[...]).astype(BF16)
    for k in range(1, ng):
        to = lax.rem(g + k, ng)
        pltpu.make_async_remote_copy(
            src_ref=hubret_send.at[to], dst_ref=hubret.at[ng - 1 - k], send_sem=sh2, recv_sem=rh2,
            device_id=(b, to), device_id_type=MESH,
        ).start()
    for r in range(row_tiles):
        own[r * TILE:(r + 1) * TILE, :] = dot(AT[r], gb[...])

    pltpu.make_async_copy(ybuf, ybuf, ar_r.at[0]).wait()
    quarter = part[pl.ds(pl.multiple_of(g * q_rows, q_rows), q_rows), :]
    for k in range(ng - 1):
        quarter = quarter + ybuf[k]
    blocks = q3.shape[1]
    wide = w.shape[1] // TILE
    for n in range(inner * blocks):
        q3[n // blocks, n % blocks] = quarter[(n // wide) * 8:(n // wide) * 8 + 8, (n % wide) * TILE:(n % wide + 1) * TILE]

    def to_inner(k, _):
        to = lax.rem(ii + k, inner)
        pltpu.make_async_remote_copy(
            src_ref=q3.at[to], dst_ref=xbuf.at[inner - 1 - k], send_sem=ar_s.at[1], recv_sem=ar_r.at[1],
            device_id=(z * inner + to, g), device_id_type=MESH,
        ).start()
        return 0

    lax.fori_loop(1, inner, to_inner, 0)
    pltpu.make_async_copy(xbuf, xbuf, ar_r.at[1]).wait()
    eighth = q3[ii]
    for k in range(inner - 1):
        eighth = eighth + xbuf[k]
    zown[...] = eighth

    def to_z(k, _):
        pltpu.make_async_remote_copy(
            src_ref=zown, dst_ref=zbuf.at[z], send_sem=ar_s.at[2], recv_sem=ar_r.at[2],
            device_id=(lax.rem(z + k, nz) * inner + ii, g), device_id_type=MESH,
        ).start()
        return 0

    lax.fori_loop(1, nz, to_z, 0)
    zbuf[z] = eighth
    if nz > 1:
        pltpu.make_async_copy(zbuf.at[pl.ds(0, nz - 1)], zbuf.at[pl.ds(0, nz - 1)], ar_r.at[2]).wait()
    total = zbuf[0]
    for k in range(1, nz):
        total = total + zbuf[k]
    f3[ii] = total
    zown2 = f3.at[ii]

    def from_inner(k, _):
        pltpu.make_async_remote_copy(
            src_ref=zown2, dst_ref=f3.at[ii], send_sem=ar_s.at[3], recv_sem=ar_r.at[3],
            device_id=(z * inner + lax.rem(ii + k, inner), g), device_id_type=MESH,
        ).start()
        return 0

    lax.fori_loop(1, inner, from_inner, 0)
    pltpu.make_async_copy(f3.at[pl.ds(0, inner - 1)], f3.at[pl.ds(0, inner - 1)], ar_r.at[3]).wait()
    wbuf[g] = f3[...]
    for k in range(1, ng):
        pltpu.make_async_remote_copy(
            src_ref=f3, dst_ref=wbuf.at[g], send_sem=ar_s.at[4], recv_sem=ar_r.at[4],
            device_id=(b, lax.rem(g + k, ng)), device_id_type=MESH,
        ).start()
    pltpu.make_async_copy(wbuf.at[pl.ds(0, ng - 1)], wbuf.at[pl.ds(0, ng - 1)], ar_r.at[4]).wait()
    for k in range(ng):
        for n in range(inner * blocks):
            top = k * q_rows + (n // wide) * 8
            wg[top:top + 8, (n % wide) * TILE:(n % wide + 1) * TILE] = wbuf[k, n // blocks, n % blocks]
    wg_out = pltpu.make_async_copy(wg, wg_h, out_sems.at[1])
    wg_out.start()

    pltpu.make_async_copy(hubret, hubret, rh2).wait()
    hub_sum = hubret_send[g].astype(F32)
    for k in range(ng - 1):
        hub_sum = hub_sum + hubret[k].astype(F32)
    hub_hi = hub_sum.astype(BF16)
    hub_lo = (hub_sum - hub_hi.astype(F32)).astype(BF16)
    own[...] = own[...] + dot(ohhubT[...], hub_hi) + dot(ohhubT[...], hub_lo)
    pltpu.make_async_copy(ret, ret, r2).wait()
    for r in range(row_tiles):
        at = slice(r * TILE, (r + 1) * TILE)
        own[at, :] = own[at, :] + dot(ohT[at, :], ret[...])
    fg_out = pltpu.make_async_copy(own, fg_h, out_sems.at[2])
    fg_out.start()

    flat = pl.ds(0, (nb - 1) * slots)
    drop = ret.at[flat]
    pltpu.make_async_copy(drop, drop, s1).wait()
    pltpu.make_async_copy(drop, drop, s2).wait()
    pltpu.make_async_copy(hubret, hubret, sh1).wait()
    pltpu.make_async_copy(hubret, hubret, sh2).wait()
    pltpu.make_async_copy(ybuf, ybuf, ar_s.at[0]).wait()
    pltpu.make_async_copy(xbuf, xbuf, ar_s.at[1]).wait()
    if nz > 1:
        pltpu.make_async_copy(zbuf.at[pl.ds(0, nz - 1)], zbuf.at[pl.ds(0, nz - 1)], ar_s.at[2]).wait()
    pltpu.make_async_copy(xbuf, xbuf, ar_s.at[3]).wait()
    pltpu.make_async_copy(wbuf.at[pl.ds(0, ng - 1)], wbuf.at[pl.ds(0, ng - 1)], ar_s.at[4]).wait()
    act_out.wait()
    wg_out.wait()
    fg_out.wait()


def body(nb, ng, features, weight, cotangent, tiles, tile_row, tile_col, hub_index, send_index, send_count):
    rows, fin = features.shape
    fout = weight.shape[1]
    tile_count = tiles.shape[0]
    slots = send_index.shape[1]
    inner = 8
    nz = nb // inner
    chunks = nb * slots // TILE
    row_tiles = rows // TILE
    src_tiles = row_tiles + chunks + ng
    idx_rows = (chunks + 8) // 8 * 8
    blocks = (TILE // ng // 8) * (fout // TILE) // inner
    vm = pltpu.VMEM
    dma = pltpu.SemaphoreType.DMA
    scratch = [
        vm((rows, fin), BF16), vm((fin, fout), BF16), vm((fout, fin), BF16), vm((rows, fout), BF16),
        vm((tile_count, TILE, TILE), BF16), vm((1, tile_count), jnp.int32), vm((1, tile_count), jnp.int32),
        vm((1, TILE), jnp.int32), vm((nb + 8, slots), jnp.int32), pltpu.SMEM((nb,), jnp.int32),
        vm((idx_rows, TILE), jnp.int32), vm((idx_rows, TILE), F32), vm((chunks, TILE, fin), BF16),
        vm((nb * slots, fin), BF16), vm((ng, TILE, fin), BF16), vm((TILE, fin), BF16),
        vm((rows, chunks * TILE), BF16), vm((rows, TILE), BF16),
        vm((8, TILE), jnp.int32), pltpu.SMEM((8, TILE), jnp.int32),
        vm((tile_count + 1, TILE, TILE), BF16), vm((tile_count + 1, TILE, TILE), BF16),
        vm((rows, src_tiles * TILE), BF16), vm((src_tiles, TILE, rows), BF16),
        vm((rows, fin), F32), vm((rows, fin), BF16), vm((rows, fout), BF16), vm((rows, fin), BF16),
        vm((rows, fout), BF16), vm((chunks, TILE, fin), BF16), vm((nb * slots, fin), BF16),
        vm((ng, TILE, fin), BF16), vm((ng - 1, TILE, fin), BF16),
        vm((fin, fout), F32), vm((ng - 1, TILE // ng, fout), F32), vm((inner, blocks, 8, TILE), F32),
        vm((inner - 1, blocks, 8, TILE), F32), vm((nz, blocks, 8, TILE), F32), vm((blocks, 8, TILE), F32),
        vm((inner, blocks, 8, TILE), F32), vm((ng, inner, blocks, 8, TILE), F32), vm((fin, fout), F32),
        vm((rows, fin), F32),
        dma((10,)), dma, dma, dma, dma, dma, dma, dma, dma, dma((5,)), dma((5,)), dma, dma((3,)),
    ]
    flops = 2 * (2 * rows * src_tiles * TILE * fin + 2 * rows * chunks * TILE * fin + 3 * rows * fin * fout)
    return pl.pallas_call(
        functools.partial(kernel, nb, ng, inner),
        out_shape=[
            jax.ShapeDtypeStruct((rows, fout), BF16),
            jax.ShapeDtypeStruct((fin, fout), F32),
            jax.ShapeDtypeStruct((rows, fin), F32),
        ],
        in_specs=[pl.BlockSpec(memory_space=pl.ANY)] * 10,
        out_specs=[pl.BlockSpec(memory_space=pl.ANY)] * 3,
        scratch_shapes=scratch,
        compiler_params=pltpu.CompilerParams(
            collective_id=0, has_side_effects=True, vmem_limit_bytes=48 * 1024 * 1024
        ),
        cost_estimate=pl.CostEstimate(flops=flops, bytes_accessed=4 * 1024 * 1024, transcendentals=rows * fout),
    )(
        features, weight, weight.T, cotangent, tiles, tile_row.reshape(1, tile_count),
        tile_col.reshape(1, tile_count), hub_index.reshape(1, TILE), send_index, send_count,
    )


def solution(mesh):
    both = ("blk", "grp")
    return jax.shard_map(
        functools.partial(body, mesh.shape["blk"], mesh.shape["grp"]),
        mesh=mesh,
        in_specs=(
            P(both, None), P(), P(both, None), P(both, None, None), P(both), P(both), P(both),
            P(both, None), P(both),
        ),
        out_specs=(P(both, None), P(), P(both, None)),
        check_vma=False,
    )
```

```python
import functools

import jax
import jax.numpy as jnp
from jax import lax
from jax.experimental import pallas as pl
from jax.experimental.pallas import tpu as pltpu
from jax.sharding import PartitionSpec as P

TILE = 128
MESH = pl.DeviceIdType.MESH
BF16 = jnp.bfloat16
F32 = jnp.float32


def dot(left, right):
    return lax.dot_general(left, right, (((1,), (0,)), ((), ())), preferred_element_type=F32)


def dot_t(left, right):
    return lax.dot_general(left, right, (((0,), (0,)), ((), ())), preferred_element_type=F32)


def iota(shape, axis):
    return lax.broadcasted_iota(jnp.int32, shape, axis)


def kernel(
    nb, ng, inner,
    feat_h, w_h, cot_h, tiles_h, trow_h, tcol_h, hub_h, sidx_h, scnt_h,
    act, wg, fg,
    feat, w, wt, cot, tiles, trow, tcol, hub, sidx_t, scnt, sidx,
    cntm, idxm, sendbuf, incoming, hubs, hubsend, ohT, ohhubT,
    info, info_s, run, runT, A, AT, agg, aggb, pg, gb, retbuf, ret, hubret_send, hubret,
    part, ybuf, q3, xbuf, zbuf, zown, f3, wbuf,
    in_sems, s1, r1, sh1, rh1, s2, r2, sh2, rh2, ar_s, ar_r, loc_sem,
):
    rows = feat.shape[0]
    row_tiles = rows // TILE
    slots = sidx_t.shape[0]
    per_chunk = TILE // slots
    chunks = nb // per_chunk
    tile_count = tiles.shape[0]
    nz = nb // inner
    halves = inner // per_chunk
    src_tiles = row_tiles + chunks + ng
    span = nz * TILE
    b = lax.axis_index("blk")
    g = lax.axis_index("grp")
    z = b // inner
    ii = lax.rem(b, inner)
    half = ii // per_chunk
    lane_dev = lax.rem(b, per_chunk)

    ins = [
        (sidx_h, sidx_t), (scnt_h, scnt), (feat_h, feat), (hub_h, hub), (trow_h, trow),
        (tcol_h, tcol), (tiles_h, tiles), (w_h, w), (cot_h, cot),
    ]
    loads = [pltpu.make_async_copy(h, v, in_sems.at[i]) for i, (h, v) in enumerate(ins)]
    for load in loads:
        load.start()

    barrier = pltpu.get_barrier_semaphore()

    def greet_blk(k, _):
        pl.semaphore_signal(barrier, inc=1, device_id=(lax.rem(b + k, nb), g), device_id_type=MESH)
        return 0

    def greet_grp(k, _):
        pl.semaphore_signal(barrier, inc=1, device_id=(b, lax.rem(g + k, ng)), device_id_type=MESH)
        return 0

    lax.fori_loop(1, nb, greet_blk, 0)
    lax.fori_loop(1, ng, greet_grp, 0)

    loads[0].wait()
    loads[1].wait()
    lane1 = iota((1, TILE), 1)
    for i in range(chunks):
        row = jnp.full((1, TILE), scnt[i * per_chunk], jnp.int32)
        for q in range(1, per_chunk):
            row = jnp.where(lane1 >= q * slots, scnt[i * per_chunk + q], row)
        cntm[i:i + 1, :] = row
    sidx[0:nb, :] = jnp.transpose(sidx_t[...])
    idx = jnp.concatenate(
        [sidx[pl.ds(q, chunks, stride=per_chunk), :] for q in range(per_chunk)], axis=1
    )
    slot_of = lax.rem(iota((chunks, TILE), 1), slots)
    idxm[0:chunks, :] = jnp.where(slot_of < cntm[0:chunks, :], idx, -1).astype(F32)
    loads[3].wait()
    idxm[chunks:chunks + 1, :] = hub[...].astype(F32)
    loads[2].wait()

    lane_rows = iota((TILE, rows), 1).astype(F32)

    def gather(row):
        column = jnp.transpose(jnp.broadcast_to(row, (TILE, TILE)))
        wide = jnp.concatenate([column] * row_tiles, axis=1)
        onehot = jnp.where(wide == lane_rows, 1.0, 0.0).astype(BF16)
        return dot(onehot, feat[...]).astype(BF16)

    rounds = [(e, q) for e in reversed(range(halves)) for q in reversed(range(per_chunk))]

    def to_z(m):
        step = (m + 1) // 2
        return lax.rem(z + jnp.where(lax.rem(m, 2) == 1, nz // 2 - step, nz - nz // 2 + step), nz)

    def to_half(e):
        return lax.rem(half + e, halves)

    mine = pl.ds(pl.multiple_of(((half * nz + z) * per_chunk + lane_dev) * slots, slots), slots)

    def exchange(buffer, landing, ssem, rsem, e, q):
        piece = lax.rem(lane_dev + q, per_chunk)

        def source(m):
            return buffer.at[e, m, pl.ds(pl.multiple_of(piece * slots, slots), slots)]

        def send(m, _):
            pltpu.make_async_remote_copy(
                src_ref=source(m), dst_ref=landing.at[mine], send_sem=ssem, recv_sem=rsem.at[e],
                device_id=((to_z(m) * halves + to_half(e)) * per_chunk + piece, g), device_id_type=MESH,
            ).start()
            return 0

        if e == 0 and q == 0:
            lax.fori_loop(0, nz - 1, send, 0)
            pltpu.make_async_copy(source(nz - 1), landing.at[mine], rsem.at[0]).start()
        else:
            lax.fori_loop(0, nz, send, 0)

    def landed(landing, rsem, e):
        some = landing.at[pl.ds(0, span)]
        pltpu.make_async_copy(some, some, rsem.at[e]).wait()
        return pl.ds(pl.multiple_of(to_half(e) * span, TILE), span)

    def gather_some(e, lo, hi):
        def at(m, _):
            sendbuf[e, m] = gather(idxm[pl.ds(to_z(m) * halves + to_half(e), 1), :])
            return 0

        lax.fori_loop(lo, hi, at, 0)

    hubsend[...] = gather(idxm[chunks:chunks + 1, :])
    hubs[g] = hubsend[...]
    gather_some(halves - 1, 0, nz)
    pl.semaphore_wait(barrier, nb - 1 + ng - 1)
    for k in range(1, ng):
        pltpu.make_async_remote_copy(
            src_ref=hubsend, dst_ref=hubs.at[g], send_sem=sh1, recv_sem=rh1,
            device_id=(b, lax.rem(g + k, ng)), device_id_type=MESH,
        ).start()

    def turns(produce, buffer, landing, ssem, rsem, between):
        for i, (e, q) in enumerate(rounds):
            exchange(buffer, landing, ssem, rsem, e, q)
            turn = i % per_chunk
            if e > 0:
                produce(e - 1, turn * nz // per_chunk, (turn + 1) * nz // per_chunk)
            between(i)

    turns(gather_some, sendbuf, incoming, s1, r1, lambda i: None)

    loads[4].wait()
    loads[5].wait()
    cells = row_tiles * src_tiles
    pad = jnp.full((1, TILE - tile_count), cells + 4, jnp.int32)
    key = jnp.concatenate([trow[...] * src_tiles + tcol[...], pad], axis=1) if tile_count < TILE else trow[...] * src_tiles + tcol[...]
    full = (TILE, TILE)
    lane = iota(full, 1)
    sub = iota(full, 0)

    def count(mask, values=1):
        return jnp.sum(jnp.where(mask, values, 0), axis=0, keepdims=True)

    key_l = jnp.broadcast_to(key, full)
    key_s = jnp.transpose(key_l)
    before = jnp.logical_or(key_s < key_l, jnp.logical_and(key_s == key_l, sub < lane))
    rank_s = jnp.transpose(jnp.broadcast_to(count(before), full))
    sorted_key = count(rank_s == lane, key_s)
    former_key = count(rank_s == lane - 1, key_s)
    first = jnp.where(jnp.logical_or(sorted_key != former_key, lane[0:1] == 0), 1, 0)
    upto = count(key_s <= lane)
    last = jnp.where(count(key_s == lane) > 0, upto - 1, tile_count)
    info[0:1, :] = jnp.clip(count(rank_s == lane, sub), 0, tile_count - 1)
    info[1:2, :] = first
    info[2:3, :] = jnp.clip(last, 0, tile_count)
    info[3:8, :] = jnp.zeros((5, TILE), jnp.int32)
    to_scalars = pltpu.make_async_copy(info, info_s, loc_sem)
    to_scalars.start()
    to_scalars.wait()

    loads[6].wait()
    run[tile_count] = jnp.zeros(full, BF16)
    runT[tile_count] = jnp.zeros(full, BF16)

    def add_tile(k, total):
        value = tiles[jnp.clip(info_s[0, k], 0, tile_count - 1)].astype(F32)
        total = jnp.where(info_s[1, k] == 1, value, total + value)
        run[k] = total.astype(BF16)
        runT[k] = jnp.transpose(total).astype(BF16)
        return total

    lax.fori_loop(0, tile_count, add_tile, jnp.zeros(full, F32))

    def place(c, _):
        bound = c - row_tiles
        moved = row_tiles + lax.rem(bound, halves) * nz + bound // halves
        within = jnp.logical_and(bound >= 0, bound < chunks)
        at = pl.ds(pl.multiple_of(jnp.where(within, moved, c) * TILE, TILE), TILE)
        for r in range(row_tiles):
            cell = jnp.clip(info_s[2, r * src_tiles + c], 0, tile_count)
            A[r * TILE:(r + 1) * TILE, at] = run[cell]
            AT[c, :, r * TILE:(r + 1) * TILE] = runT[cell]
        return 0

    lax.fori_loop(0, src_tiles, place, 0)

    sub_rows = iota((rows, TILE), 0).astype(F32)

    def columns(i, _):
        row = idxm[pl.ds(i, 1), :]
        place_at = lax.rem(i, halves) * nz + i // halves
        ohT[:, pl.ds(pl.multiple_of(place_at * TILE, TILE), TILE)] = jnp.where(sub_rows == row, 1.0, 0.0).astype(BF16)
        return 0

    lax.fori_loop(0, chunks, columns, 0)
    ohhubT[...] = jnp.where(sub_rows == idxm[chunks:chunks + 1, :], 1.0, 0.0).astype(BF16)

    lo, hi = rows, rows + chunks * TILE
    pltpu.make_async_copy(hubs.at[pl.ds(0, ng - 1)], hubs.at[pl.ds(0, ng - 1)], rh1).wait()
    agg[...] = dot(A[:, 0:lo], feat[...]) + dot(A[:, hi:], hubs[...].reshape(ng * TILE, TILE))
    for i in range(7, 9):
        loads[i].wait()
    wt[...] = jnp.transpose(w[...].astype(F32)).astype(BF16)

    for e in reversed(range(halves)):
        at = landed(incoming, r1, e)
        columns_at = pl.ds(pl.multiple_of(lo + to_half(e) * span, TILE), span)
        agg[...] = agg[...] + dot(A[:, columns_at], incoming[at, :])
    for r in range(row_tiles):
        at = slice(r * TILE, (r + 1) * TILE)
        summed = agg[at, :].astype(BF16)
        aggb[at, :] = summed
        preact = dot(summed, w[...])
        logistic = 1.0 / (1.0 + jnp.exp(-preact))
        act[at, :] = (preact * logistic).astype(BF16)
        grad = (cot[at, :].astype(F32) * (logistic * (1.0 + preact * (1.0 - logistic)))).astype(BF16)
        pg[at, :] = grad
        gb[at, :] = dot(grad, wt[...]).astype(BF16)

    part[...] = dot_t(aggb[...], pg[...])
    q_rows = TILE // ng

    def q_of(k):
        return part.at[pl.ds(pl.multiple_of(k * q_rows, q_rows), q_rows)]

    for k in range(1, ng):
        to = lax.rem(g + k, ng)
        pltpu.make_async_remote_copy(
            src_ref=q_of(to), dst_ref=ybuf.at[ng - 1 - k], send_sem=ar_s.at[0], recv_sem=ar_r.at[0],
            device_id=(b, to), device_id_type=MESH,
        ).start()

    blocks = q3.shape[1]
    wide = w.shape[1] // TILE
    most = pl.ds(0, inner - 1)

    def over_inner():
        pltpu.make_async_copy(ybuf, ybuf, ar_r.at[0]).wait()
        quarter = part[pl.ds(pl.multiple_of(g * q_rows, q_rows), q_rows), :]
        for k in range(ng - 1):
            quarter = quarter + ybuf[k]
        for n in range(inner * blocks):
            q3[n // blocks, n % blocks] = quarter[
                (n // wide) * 8:(n // wide) * 8 + 8, (n % wide) * TILE:(n % wide + 1) * TILE
            ]

        def to_inner(k, _):
            to = lax.rem(ii + k, inner)
            pltpu.make_async_remote_copy(
                src_ref=q3.at[to], dst_ref=xbuf.at[inner - 1 - k], send_sem=ar_s.at[1], recv_sem=ar_r.at[1],
                device_id=(z * inner + to, g), device_id_type=MESH,
            ).start()
            return 0

        lax.fori_loop(1, inner, to_inner, 0)

    def over_z():
        pltpu.make_async_copy(xbuf, xbuf, ar_r.at[1]).wait()
        eighth = q3[ii]
        for k in range(inner - 1):
            eighth = eighth + xbuf[k]
        zown[...] = eighth
        zbuf[z] = eighth

        def send_z(k, _):
            pltpu.make_async_remote_copy(
                src_ref=zown, dst_ref=zbuf.at[z], send_sem=ar_s.at[2], recv_sem=ar_r.at[2],
                device_id=(lax.rem(z + k, nz) * inner + ii, g), device_id_type=MESH,
            ).start()
            return 0

        lax.fori_loop(1, nz, send_z, 0)

    def back_inner():
        others = zbuf.at[pl.ds(0, nz - 1)]
        pltpu.make_async_copy(others, others, ar_r.at[2]).wait()
        total = zbuf[0]
        for k in range(1, nz):
            total = total + zbuf[k]
        f3[ii] = total

        def from_inner(k, _):
            pltpu.make_async_remote_copy(
                src_ref=f3.at[ii], dst_ref=f3.at[ii], send_sem=ar_s.at[3], recv_sem=ar_r.at[3],
                device_id=(z * inner + lax.rem(ii + k, inner), g), device_id_type=MESH,
            ).start()
            return 0

        lax.fori_loop(1, inner, from_inner, 0)

    def back_grp():
        pltpu.make_async_copy(f3.at[most], f3.at[most], ar_r.at[3]).wait()
        wbuf[g] = f3[...]
        for k in range(1, ng):
            pltpu.make_async_remote_copy(
                src_ref=f3, dst_ref=wbuf.at[g], send_sem=ar_s.at[4], recv_sem=ar_r.at[4],
                device_id=(b, lax.rem(g + k, ng)), device_id_type=MESH,
            ).start()

    def finish_weight():
        others = wbuf.at[pl.ds(0, ng - 1)]
        pltpu.make_async_copy(others, others, ar_r.at[4]).wait()
        for k in range(ng):
            for n in range(inner * blocks):
                top = k * q_rows + (n // wide) * 8
                wg[top:top + 8, (n % wide) * TILE:(n % wide + 1) * TILE] = wbuf[k, n // blocks, n % blocks]

    def back_some(e, lo, hi):
        def at(m, _):
            retbuf[e, m] = dot(AT[row_tiles + to_z(m) * halves + to_half(e)], gb[...]).astype(BF16)
            return 0

        lax.fori_loop(lo, hi, at, 0)

    def back_hubs():
        for k in range(ng):
            hubret_send[k] = dot(AT[row_tiles + chunks + k], gb[...]).astype(BF16)
        for k in range(1, ng):
            to = lax.rem(g + k, ng)
            pltpu.make_async_remote_copy(
                src_ref=hubret_send.at[to], dst_ref=hubret.at[ng - 1 - k], send_sem=sh2, recv_sem=rh2,
                device_id=(b, to), device_id_type=MESH,
            ).start()

    plan = {1: over_z, 2: back_hubs, 3: back_inner, 5: back_grp}
    back_some(halves - 1, 0, nz)
    over_inner()
    turns(back_some, retbuf, ret, s2, r2, lambda i: plan.get(i, lambda: None)())
    for r in range(row_tiles):
        fg[r * TILE:(r + 1) * TILE, :] = dot(AT[r], gb[...])
    finish_weight()

    pltpu.make_async_copy(hubret, hubret, rh2).wait()
    hub_sum = hubret_send[g].astype(F32)
    for k in range(ng - 1):
        hub_sum = hub_sum + hubret[k].astype(F32)
    hub_hi = hub_sum.astype(BF16)
    hub_lo = (hub_sum - hub_hi.astype(F32)).astype(BF16)
    fg[...] = fg[...] + dot(ohhubT[...], hub_hi) + dot(ohhubT[...], hub_lo)
    for e in reversed(range(halves)):
        at = landed(ret, r2, e)
        fg[...] = fg[...] + dot(ohT[:, at], ret[at, :])

    flat = pl.ds(0, (nb - 1) * slots)
    drop = ret.at[flat]
    pltpu.make_async_copy(drop, drop, s1).wait()
    pltpu.make_async_copy(drop, drop, s2).wait()
    pltpu.make_async_copy(hubret, hubret, sh1).wait()
    pltpu.make_async_copy(hubret, hubret, sh2).wait()
    pltpu.make_async_copy(ybuf, ybuf, ar_s.at[0]).wait()
    pltpu.make_async_copy(xbuf, xbuf, ar_s.at[1]).wait()
    pltpu.make_async_copy(zbuf.at[pl.ds(0, nz - 1)], zbuf.at[pl.ds(0, nz - 1)], ar_s.at[2]).wait()
    pltpu.make_async_copy(xbuf, xbuf, ar_s.at[3]).wait()
    pltpu.make_async_copy(wbuf.at[pl.ds(0, ng - 1)], wbuf.at[pl.ds(0, ng - 1)], ar_s.at[4]).wait()


def hand_out(a, b, c, a_out, b_out, c_out, sems):
    copies = [
        pltpu.make_async_copy(source, target, sems.at[i])
        for i, (source, target) in enumerate([(a, a_out), (b, b_out), (c, c_out)])
    ]
    for copy in copies:
        copy.start()
    for copy in copies:
        copy.wait()


def body(nb, ng, features, weight, cotangent, tiles, tile_row, tile_col, hub_index, send_index, send_count):
    rows, fin = features.shape
    fout = weight.shape[1]
    tile_count = tiles.shape[0]
    slots = send_index.shape[1]
    inner = 8
    nz = nb // inner
    chunks = nb * slots // TILE
    row_tiles = rows // TILE
    src_tiles = row_tiles + chunks + ng
    idx_rows = (chunks + 8) // 8 * 8
    blocks = (TILE // ng // 8) * (fout // TILE) // inner
    vm = pltpu.VMEM
    dma = pltpu.SemaphoreType.DMA
    scratch = [
        vm((rows, fin), BF16), vm((fin, fout), BF16), vm((fout, fin), BF16), vm((rows, fout), BF16),
        vm((tile_count, TILE, TILE), BF16), vm((1, tile_count), jnp.int32), vm((1, tile_count), jnp.int32),
        vm((1, TILE), jnp.int32), vm((slots, nb), jnp.int32), pltpu.SMEM((nb,), jnp.int32),
        vm((nb + 8, slots), jnp.int32),
        vm((idx_rows, TILE), jnp.int32), vm((idx_rows, TILE), F32), vm((2, nz, TILE, fin), BF16),
        vm((nb * slots, fin), BF16), vm((ng, TILE, fin), BF16), vm((TILE, fin), BF16),
        vm((rows, chunks * TILE), BF16), vm((rows, TILE), BF16),
        vm((8, TILE), jnp.int32), pltpu.SMEM((8, TILE), jnp.int32),
        vm((tile_count + 1, TILE, TILE), BF16), vm((tile_count + 1, TILE, TILE), BF16),
        vm((rows, src_tiles * TILE), BF16), vm((src_tiles, TILE, rows), BF16),
        vm((rows, fin), F32), vm((rows, fin), BF16), vm((rows, fout), BF16), vm((rows, fin), BF16),
        vm((2, nz, TILE, fin), BF16), vm((nb * slots, fin), BF16),
        vm((ng, TILE, fin), BF16), vm((ng - 1, TILE, fin), BF16),
        vm((fin, fout), F32), vm((ng - 1, TILE // ng, fout), F32), vm((inner, blocks, 8, TILE), F32),
        vm((inner - 1, blocks, 8, TILE), F32), vm((nz, blocks, 8, TILE), F32), vm((blocks, 8, TILE), F32),
        vm((inner, blocks, 8, TILE), F32), vm((ng, inner, blocks, 8, TILE), F32),
        dma((9,)), dma, dma((2,)), dma, dma, dma, dma((2,)), dma, dma, dma((5,)), dma((5,)), dma,
    ]
    flops = 2 * (2 * rows * src_tiles * TILE * fin + 2 * rows * chunks * TILE * fin + 3 * rows * fin * fout)
    results = pl.pallas_call(
        functools.partial(kernel, nb, ng, inner),
        out_shape=[vm((rows, fout), BF16), vm((fin, fout), F32), vm((rows, fin), F32)],
        in_specs=[pl.BlockSpec(memory_space=pl.ANY)] * 9,
        out_specs=[pl.BlockSpec(memory_space=pltpu.VMEM)] * 3,
        scratch_shapes=scratch,
        compiler_params=pltpu.CompilerParams(
            collective_id=0, has_side_effects=True, vmem_limit_bytes=56 * 1024 * 1024
        ),
        cost_estimate=pl.CostEstimate(flops=flops, bytes_accessed=4 * 1024 * 1024, transcendentals=rows * fout),
    )(
        features, weight, cotangent, tiles, tile_row.reshape(1, tile_count),
        tile_col.reshape(1, tile_count), hub_index.reshape(1, TILE), send_index.T, send_count,
    )
    return pl.pallas_call(
        hand_out,
        out_shape=[jax.ShapeDtypeStruct(result.shape, result.dtype) for result in results],
        in_specs=[pl.BlockSpec(memory_space=pl.ANY)] * 3,
        out_specs=[pl.BlockSpec(memory_space=pl.ANY)] * 3,
        scratch_shapes=[dma((3,))],
        compiler_params=pltpu.CompilerParams(vmem_limit_bytes=1024 * 1024),
    )(*results)


def solution(mesh):
    both = ("blk", "grp")
    return jax.shard_map(
        functools.partial(body, mesh.shape["blk"], mesh.shape["grp"]),
        mesh=mesh,
        in_specs=(
            P(both, None), P(), P(both, None), P(both, None, None), P(both), P(both), P(both),
            P(both, None), P(both),
        ),
        out_specs=(P(both, None), P(), P(both, None)),
        check_vma=False,
    )
```

```python
import functools

import jax
import jax.numpy as jnp
from jax import lax
from jax.experimental import pallas as pl
from jax.experimental.pallas import tpu as pltpu
from jax.sharding import PartitionSpec as P

TILE = 128
MESH = pl.DeviceIdType.MESH
BF16 = jnp.bfloat16
F32 = jnp.float32


def dot(left, right):
    return lax.dot_general(left, right, (((1,), (0,)), ((), ())), preferred_element_type=F32)


def dot_t(left, right):
    return lax.dot_general(left, right, (((0,), (0,)), ((), ())), preferred_element_type=F32)


def iota(shape, axis):
    return lax.broadcasted_iota(jnp.int32, shape, axis)


def kernel(
    nb, ng, inner,
    feat_h, w_h, cot_h, tiles_h, trow_h, tcol_h, hub_h, sidx_h, scnt_h,
    act, wg, fg,
    feat, w, wt, cot, tiles, trow, tcol, hub, sidx_t, scnt, sidx,
    cntm, idxm, sendbuf, incoming, hubs, hubsend, ohT, ohhubT,
    info, info_s, run, runT, A, AT, agg, aggb, pg, gb, retbuf, ret, hubret_send, hubret,
    part, q3, xbuf, zbuf, zown, f3,
    in_sems, s1, r1, sh1, rh1, s2, r2, sh2, rh2, ar_s, ar_r, loc_sem,
):
    rows = feat.shape[0]
    row_tiles = rows // TILE
    slots = sidx_t.shape[0]
    per_chunk = TILE // slots
    chunks = nb // per_chunk
    tile_count = tiles.shape[0]
    nz = nb // inner
    halves = inner // per_chunk
    src_tiles = row_tiles + chunks + ng
    span = nz * TILE
    b = lax.axis_index("blk")
    g = lax.axis_index("grp")
    z = b // inner
    ii = lax.rem(b, inner)
    half = ii // per_chunk
    lane_dev = lax.rem(b, per_chunk)
    u = g * inner + ii

    ins = [
        (sidx_h, sidx_t), (scnt_h, scnt), (feat_h, feat), (hub_h, hub), (trow_h, trow),
        (tcol_h, tcol), (tiles_h, tiles), (w_h, w), (cot_h, cot),
    ]
    loads = [pltpu.make_async_copy(h, v, in_sems.at[i]) for i, (h, v) in enumerate(ins)]
    for load in loads:
        load.start()

    barrier = pltpu.get_barrier_semaphore()

    def greet_z(k, _):
        to = lax.rem(z * inner + k, nb)
        pl.semaphore_signal(barrier, inc=1, device_id=(to, g), device_id_type=MESH)
        return 0

    def greet_grp(k, _):
        to = lax.rem(u + k, ng * inner)
        pl.semaphore_signal(barrier, inc=1, device_id=(z * inner + lax.rem(to, inner), to // inner), device_id_type=MESH)
        return 0

    others = nb - inner + ng * inner - 1

    lax.fori_loop(inner, nb, greet_z, 0)
    lax.fori_loop(1, ng * inner, greet_grp, 0)

    loads[0].wait()
    loads[1].wait()
    lane1 = iota((1, TILE), 1)
    for i in range(chunks):
        row = jnp.full((1, TILE), scnt[i * per_chunk], jnp.int32)
        for q in range(1, per_chunk):
            row = jnp.where(lane1 >= q * slots, scnt[i * per_chunk + q], row)
        cntm[i:i + 1, :] = row
    sidx[0:nb, :] = jnp.transpose(sidx_t[...])
    idx = jnp.concatenate(
        [sidx[pl.ds(q, chunks, stride=per_chunk), :] for q in range(per_chunk)], axis=1
    )
    slot_of = lax.rem(iota((chunks, TILE), 1), slots)
    idxm[0:chunks, :] = jnp.where(slot_of < cntm[0:chunks, :], idx, -1).astype(F32)
    loads[3].wait()
    idxm[chunks:chunks + 1, :] = hub[...].astype(F32)
    loads[2].wait()

    lane_rows = iota((TILE, rows), 1).astype(F32)

    def gather(row):
        column = jnp.transpose(jnp.broadcast_to(row, (TILE, TILE)))
        wide = jnp.concatenate([column] * row_tiles, axis=1)
        onehot = jnp.where(wide == lane_rows, 1.0, 0.0).astype(BF16)
        return dot(onehot, feat[...]).astype(BF16)

    rounds = [(e, q) for e in reversed(range(halves)) for q in reversed(range(per_chunk))]

    def to_z(m):
        step = (m + 1) // 2
        return lax.rem(z + jnp.where(lax.rem(m, 2) == 1, nz // 2 - step, nz - nz // 2 + step), nz)

    def to_half(e):
        return lax.rem(half + e, halves)

    mine = pl.ds(pl.multiple_of(((half * nz + z) * per_chunk + lane_dev) * slots, slots), slots)

    def exchange(buffer, landing, ssem, rsem, e, q):
        piece = lax.rem(lane_dev + q, per_chunk)

        def source(m):
            return buffer.at[e, m, pl.ds(pl.multiple_of(piece * slots, slots), slots)]

        def send(m, _):
            pltpu.make_async_remote_copy(
                src_ref=source(m), dst_ref=landing.at[mine], send_sem=ssem, recv_sem=rsem.at[e],
                device_id=((to_z(m) * halves + to_half(e)) * per_chunk + piece, g), device_id_type=MESH,
            ).start()
            return 0

        if e == 0 and q == 0:
            lax.fori_loop(0, nz - 1, send, 0)
            pltpu.make_async_copy(source(nz - 1), landing.at[mine], rsem.at[0]).start()
        else:
            lax.fori_loop(0, nz, send, 0)

    def landed(landing, rsem, e):
        some = landing.at[pl.ds(0, span)]
        pltpu.make_async_copy(some, some, rsem.at[e]).wait()
        return pl.ds(pl.multiple_of(to_half(e) * span, TILE), span)

    def gather_some(e, lo, hi):
        def at(m, _):
            sendbuf[e, m] = gather(idxm[pl.ds(to_z(m) * halves + to_half(e), 1), :])
            return 0

        lax.fori_loop(lo, hi, at, 0)

    hubsend[...] = gather(idxm[chunks:chunks + 1, :])
    hubs[g] = hubsend[...]
    gather_some(halves - 1, 0, nz)
    pl.semaphore_wait(barrier, others)
    for k in range(1, ng):
        pltpu.make_async_remote_copy(
            src_ref=hubsend, dst_ref=hubs.at[g], send_sem=sh1, recv_sem=rh1,
            device_id=(b, lax.rem(g + k, ng)), device_id_type=MESH,
        ).start()

    def turns(produce, buffer, landing, ssem, rsem, between):
        for i, (e, q) in enumerate(rounds):
            exchange(buffer, landing, ssem, rsem, e, q)
            turn = i % per_chunk
            if e > 0:
                produce(e - 1, turn * nz // per_chunk, (turn + 1) * nz // per_chunk)
            between(i)

    turns(gather_some, sendbuf, incoming, s1, r1, lambda i: None)

    loads[4].wait()
    loads[5].wait()
    cells = row_tiles * src_tiles
    pad = jnp.full((1, TILE - tile_count), cells + 4, jnp.int32)
    key = jnp.concatenate([trow[...] * src_tiles + tcol[...], pad], axis=1) if tile_count < TILE else trow[...] * src_tiles + tcol[...]
    full = (TILE, TILE)
    lane = iota(full, 1)
    sub = iota(full, 0)

    def count(mask, values=1):
        return jnp.sum(jnp.where(mask, values, 0), axis=0, keepdims=True)

    key_l = jnp.broadcast_to(key, full)
    key_s = jnp.transpose(key_l)
    before = jnp.logical_or(key_s < key_l, jnp.logical_and(key_s == key_l, sub < lane))
    rank_s = jnp.transpose(jnp.broadcast_to(count(before), full))
    sorted_key = count(rank_s == lane, key_s)
    former_key = count(rank_s == lane - 1, key_s)
    first = jnp.where(jnp.logical_or(sorted_key != former_key, lane[0:1] == 0), 1, 0)
    upto = count(key_s <= lane)
    last = jnp.where(count(key_s == lane) > 0, upto - 1, tile_count)
    info[0:1, :] = jnp.clip(count(rank_s == lane, sub), 0, tile_count - 1)
    info[1:2, :] = first
    info[2:3, :] = jnp.clip(last, 0, tile_count)
    info[3:8, :] = jnp.zeros((5, TILE), jnp.int32)
    to_scalars = pltpu.make_async_copy(info, info_s, loc_sem)
    to_scalars.start()
    to_scalars.wait()

    loads[6].wait()
    run[tile_count] = jnp.zeros(full, BF16)
    runT[tile_count] = jnp.zeros(full, BF16)

    def add_tile(k, total):
        value = tiles[jnp.clip(info_s[0, k], 0, tile_count - 1)].astype(F32)
        total = jnp.where(info_s[1, k] == 1, value, total + value)
        run[k] = total.astype(BF16)
        runT[k] = jnp.transpose(total).astype(BF16)
        return total

    lax.fori_loop(0, tile_count, add_tile, jnp.zeros(full, F32))

    def place(c, _):
        bound = c - row_tiles
        moved = row_tiles + lax.rem(bound, halves) * nz + bound // halves
        within = jnp.logical_and(bound >= 0, bound < chunks)
        at = pl.ds(pl.multiple_of(jnp.where(within, moved, c) * TILE, TILE), TILE)
        for r in range(row_tiles):
            cell = jnp.clip(info_s[2, r * src_tiles + c], 0, tile_count)
            A[r * TILE:(r + 1) * TILE, at] = run[cell]
            AT[c, :, r * TILE:(r + 1) * TILE] = runT[cell]
        return 0

    lax.fori_loop(0, src_tiles, place, 0)

    sub_rows = iota((rows, TILE), 0).astype(F32)

    def columns(i, _):
        row = idxm[pl.ds(i, 1), :]
        place_at = lax.rem(i, halves) * nz + i // halves
        ohT[:, pl.ds(pl.multiple_of(place_at * TILE, TILE), TILE)] = jnp.where(sub_rows == row, 1.0, 0.0).astype(BF16)
        return 0

    lax.fori_loop(0, chunks, columns, 0)
    ohhubT[...] = jnp.where(sub_rows == idxm[chunks:chunks + 1, :], 1.0, 0.0).astype(BF16)

    lo, hi = rows, rows + chunks * TILE
    pltpu.make_async_copy(hubs.at[pl.ds(0, ng - 1)], hubs.at[pl.ds(0, ng - 1)], rh1).wait()
    agg[...] = dot(A[:, 0:lo], feat[...]) + dot(A[:, hi:], hubs[...].reshape(ng * TILE, TILE))
    for i in range(7, 9):
        loads[i].wait()
    wt[...] = jnp.transpose(w[...].astype(F32)).astype(BF16)

    for e in reversed(range(halves)):
        at = landed(incoming, r1, e)
        columns_at = pl.ds(pl.multiple_of(lo + to_half(e) * span, TILE), span)
        agg[...] = agg[...] + dot(A[:, columns_at], incoming[at, :])
    for r in range(row_tiles):
        at = slice(r * TILE, (r + 1) * TILE)
        summed = agg[at, :].astype(BF16)
        aggb[at, :] = summed
        preact = dot(summed, w[...])
        logistic = 1.0 / (1.0 + jnp.exp(-preact))
        act[at, :] = (preact * logistic).astype(BF16)
        grad = (cot[at, :].astype(F32) * (logistic * (1.0 + preact * (1.0 - logistic)))).astype(BF16)
        pg[at, :] = grad
        gb[at, :] = dot(grad, wt[...]).astype(BF16)

    part[...] = dot_t(aggb[...], pg[...])
    members, blocks = q3.shape[0], q3.shape[1]
    wide = w.shape[1] // TILE
    for n in range(members * blocks):
        q3[n // blocks, n % blocks] = part[(n // wide) * 8:(n // wide) * 8 + 8, (n % wide) * TILE:(n % wide + 1) * TILE]

    def over_plane(source, target, i):
        def send(k, _):
            to = lax.rem(u + k, members)
            pltpu.make_async_remote_copy(
                src_ref=source(to), dst_ref=target(k), send_sem=ar_s.at[i], recv_sem=ar_r.at[i],
                device_id=(z * inner + lax.rem(to, inner), to // inner), device_id_type=MESH,
            ).start()
            return 0

        lax.fori_loop(1, members, send, 0)

    over_plane(lambda to: q3.at[to], lambda k: xbuf.at[members - 1 - k], 0)

    def over_z():
        pltpu.make_async_copy(xbuf, xbuf, ar_r.at[0]).wait()
        summed = q3[u]
        for k in range(members - 1):
            summed = summed + xbuf[k]
        zown[...] = summed
        zbuf[z] = summed

        def send_z(k, _):
            pltpu.make_async_remote_copy(
                src_ref=zown, dst_ref=zbuf.at[z], send_sem=ar_s.at[1], recv_sem=ar_r.at[1],
                device_id=(lax.rem(z + k, nz) * inner + ii, g), device_id_type=MESH,
            ).start()
            return 0

        lax.fori_loop(1, nz, send_z, 0)

    def back_plane():
        others = zbuf.at[pl.ds(0, nz - 1)]
        pltpu.make_async_copy(others, others, ar_r.at[1]).wait()
        total = zbuf[0]
        for k in range(1, nz):
            total = total + zbuf[k]
        f3[u] = total
        over_plane(lambda to: f3.at[u], lambda k: f3.at[u], 2)

    def finish_weight():
        others = f3.at[pl.ds(0, members - 1)]
        pltpu.make_async_copy(others, others, ar_r.at[2]).wait()
        for n in range(members * blocks):
            wg[(n // wide) * 8:(n // wide) * 8 + 8, (n % wide) * TILE:(n % wide + 1) * TILE] = f3[n // blocks, n % blocks]

    def back_some(e, lo, hi):
        def at(m, _):
            retbuf[e, m] = dot(AT[row_tiles + to_z(m) * halves + to_half(e)], gb[...]).astype(BF16)
            return 0

        lax.fori_loop(lo, hi, at, 0)

    def back_hubs():
        for k in range(ng):
            hubret_send[k] = dot(AT[row_tiles + chunks + k], gb[...]).astype(BF16)
        for k in range(1, ng):
            to = lax.rem(g + k, ng)
            pltpu.make_async_remote_copy(
                src_ref=hubret_send.at[to], dst_ref=hubret.at[ng - 1 - k], send_sem=sh2, recv_sem=rh2,
                device_id=(b, to), device_id_type=MESH,
            ).start()

    plan = {0: back_hubs, 2: over_z, 5: back_plane}
    back_some(halves - 1, 0, nz)
    turns(back_some, retbuf, ret, s2, r2, lambda i: plan.get(i, lambda: None)())
    for r in range(row_tiles):
        fg[r * TILE:(r + 1) * TILE, :] = dot(AT[r], gb[...])

    pltpu.make_async_copy(hubret, hubret, rh2).wait()
    hub_sum = hubret_send[g].astype(F32)
    for k in range(ng - 1):
        hub_sum = hub_sum + hubret[k].astype(F32)
    hub_hi = hub_sum.astype(BF16)
    hub_lo = (hub_sum - hub_hi.astype(F32)).astype(BF16)
    fg[...] = fg[...] + dot(ohhubT[...], hub_hi) + dot(ohhubT[...], hub_lo)
    for e in reversed(range(halves)):
        at = landed(ret, r2, e)
        fg[...] = fg[...] + dot(ohT[:, at], ret[at, :])
    finish_weight()

    flat = pl.ds(0, (nb - 1) * slots)
    drop = ret.at[flat]
    pltpu.make_async_copy(drop, drop, s1).wait()
    pltpu.make_async_copy(drop, drop, s2).wait()
    pltpu.make_async_copy(hubret, hubret, sh1).wait()
    pltpu.make_async_copy(hubret, hubret, sh2).wait()
    others = zbuf.at[pl.ds(0, nz - 1)]
    pltpu.make_async_copy(xbuf, xbuf, ar_s.at[0]).wait()
    pltpu.make_async_copy(others, others, ar_s.at[1]).wait()
    pltpu.make_async_copy(xbuf, xbuf, ar_s.at[2]).wait()


def hand_out(a, b, c, a_out, b_out, c_out, sems):
    copies = [
        pltpu.make_async_copy(source, target, sems.at[i])
        for i, (source, target) in enumerate([(a, a_out), (b, b_out), (c, c_out)])
    ]
    for copy in copies:
        copy.start()
    for copy in copies:
        copy.wait()


def body(nb, ng, features, weight, cotangent, tiles, tile_row, tile_col, hub_index, send_index, send_count):
    rows, fin = features.shape
    fout = weight.shape[1]
    tile_count = tiles.shape[0]
    slots = send_index.shape[1]
    inner = 8
    nz = nb // inner
    chunks = nb * slots // TILE
    row_tiles = rows // TILE
    src_tiles = row_tiles + chunks + ng
    idx_rows = (chunks + 8) // 8 * 8
    members = ng * inner
    blocks = (fin // 8) * (fout // TILE) // members
    vm = pltpu.VMEM
    dma = pltpu.SemaphoreType.DMA
    scratch = [
        vm((rows, fin), BF16), vm((fin, fout), BF16), vm((fout, fin), BF16), vm((rows, fout), BF16),
        vm((tile_count, TILE, TILE), BF16), vm((1, tile_count), jnp.int32), vm((1, tile_count), jnp.int32),
        vm((1, TILE), jnp.int32), vm((slots, nb), jnp.int32), pltpu.SMEM((nb,), jnp.int32),
        vm((nb + 8, slots), jnp.int32),
        vm((idx_rows, TILE), jnp.int32), vm((idx_rows, TILE), F32), vm((2, nz, TILE, fin), BF16),
        vm((nb * slots, fin), BF16), vm((ng, TILE, fin), BF16), vm((TILE, fin), BF16),
        vm((rows, chunks * TILE), BF16), vm((rows, TILE), BF16),
        vm((8, TILE), jnp.int32), pltpu.SMEM((8, TILE), jnp.int32),
        vm((tile_count + 1, TILE, TILE), BF16), vm((tile_count + 1, TILE, TILE), BF16),
        vm((rows, src_tiles * TILE), BF16), vm((src_tiles, TILE, rows), BF16),
        vm((rows, fin), F32), vm((rows, fin), BF16), vm((rows, fout), BF16), vm((rows, fin), BF16),
        vm((2, nz, TILE, fin), BF16), vm((nb * slots, fin), BF16),
        vm((ng, TILE, fin), BF16), vm((ng - 1, TILE, fin), BF16),
        vm((fin, fout), F32), vm((members, blocks, 8, TILE), F32), vm((members - 1, blocks, 8, TILE), F32),
        vm((nz, blocks, 8, TILE), F32), vm((blocks, 8, TILE), F32), vm((members, blocks, 8, TILE), F32),
        dma((9,)), dma, dma((2,)), dma, dma, dma, dma((2,)), dma, dma, dma((3,)), dma((3,)), dma,
    ]
    flops = 2 * (2 * rows * src_tiles * TILE * fin + 2 * rows * chunks * TILE * fin + 3 * rows * fin * fout)
    results = pl.pallas_call(
        functools.partial(kernel, nb, ng, inner),
        out_shape=[vm((rows, fout), BF16), vm((fin, fout), F32), vm((rows, fin), F32)],
        in_specs=[pl.BlockSpec(memory_space=pl.ANY)] * 9,
        out_specs=[pl.BlockSpec(memory_space=pltpu.VMEM)] * 3,
        scratch_shapes=scratch,
        compiler_params=pltpu.CompilerParams(
            collective_id=0, has_side_effects=True, vmem_limit_bytes=56 * 1024 * 1024
        ),
        cost_estimate=pl.CostEstimate(flops=flops, bytes_accessed=4 * 1024 * 1024, transcendentals=rows * fout),
    )(
        features, weight, cotangent, tiles, tile_row.reshape(1, tile_count),
        tile_col.reshape(1, tile_count), hub_index.reshape(1, TILE), send_index.T, send_count,
    )
    return pl.pallas_call(
        hand_out,
        out_shape=[jax.ShapeDtypeStruct(result.shape, result.dtype) for result in results],
        in_specs=[pl.BlockSpec(memory_space=pl.ANY)] * 3,
        out_specs=[pl.BlockSpec(memory_space=pl.ANY)] * 3,
        scratch_shapes=[dma((3,))],
        compiler_params=pltpu.CompilerParams(vmem_limit_bytes=1024 * 1024),
    )(*results)


def solution(mesh):
    both = ("blk", "grp")
    return jax.shard_map(
        functools.partial(body, mesh.shape["blk"], mesh.shape["grp"]),
        mesh=mesh,
        in_specs=(
            P(both, None), P(), P(both, None), P(both, None, None), P(both), P(both), P(both),
            P(both, None), P(both),
        ),
        out_specs=(P(both, None), P(), P(both, None)),
        check_vma=False,
    )
```

```python
import functools

import jax
import jax.numpy as jnp
from jax import lax
from jax.experimental import pallas as pl
from jax.experimental.pallas import tpu as pltpu
from jax.sharding import PartitionSpec as P

TILE = 128
MESH = pl.DeviceIdType.MESH
BF16 = jnp.bfloat16
F32 = jnp.float32


def dot(left, right):
    return lax.dot_general(left, right, (((1,), (0,)), ((), ())), preferred_element_type=F32)


def dot_t(left, right):
    return lax.dot_general(left, right, (((0,), (0,)), ((), ())), preferred_element_type=F32)


def iota(shape, axis):
    return lax.broadcasted_iota(jnp.int32, shape, axis)


def kernel(
    nb, ng, inner,
    feat_h, w_h, cot_h, tiles_h, trow_h, tcol_h, hub_h, sidx_h, scnt_h,
    act, wg, fg,
    feat, w, wt, cot, tiles, trow, tcol, hub, sidx_t, scnt, sidx,
    cntm, idxm, sendbuf, incoming, hubs, hubsend, ohT, ohhubT,
    info, info_s, run, runT, A, AT, agg, aggb, pg, gb, retbuf, ret, hubret_send, hubret,
    part, q3, xbuf, zbuf, zown, f3,
    in_sems, s1, r1, sh1, rh1, s2, r2, sh2, rh2, ar_s, ar_r, loc_sem,
):
    rows = feat.shape[0]
    row_tiles = rows // TILE
    slots = sidx_t.shape[0]
    per_chunk = TILE // slots
    chunks = nb // per_chunk
    tile_count = tiles.shape[0]
    nz = nb // inner
    halves = inner // per_chunk
    src_tiles = row_tiles + chunks + ng
    span = nz * TILE
    b = lax.axis_index("blk")
    g = lax.axis_index("grp")
    z = b // inner
    ii = lax.rem(b, inner)
    half = ii // per_chunk
    lane_dev = lax.rem(b, per_chunk)
    u = g * inner + ii

    ins = [
        (sidx_h, sidx_t), (scnt_h, scnt), (feat_h, feat), (hub_h, hub), (trow_h, trow),
        (tcol_h, tcol), (tiles_h, tiles), (w_h, w), (cot_h, cot),
    ]
    loads = [pltpu.make_async_copy(h, v, in_sems.at[i]) for i, (h, v) in enumerate(ins)]
    for load in loads:
        load.start()

    barrier = pltpu.get_barrier_semaphore()

    def greet_z(k, _):
        to = lax.rem(z * inner + k, nb)
        pl.semaphore_signal(barrier, inc=1, device_id=(to, g), device_id_type=MESH)
        return 0

    def greet_grp(k, _):
        to = lax.rem(u + k, ng * inner)
        pl.semaphore_signal(barrier, inc=1, device_id=(z * inner + lax.rem(to, inner), to // inner), device_id_type=MESH)
        return 0

    greeted = nb - inner + ng * inner - 1
    lax.fori_loop(inner, nb, greet_z, 0)
    lax.fori_loop(1, ng * inner, greet_grp, 0)

    loads[0].wait()
    loads[1].wait()
    lane1 = iota((1, TILE), 1)
    for i in range(chunks):
        row = jnp.full((1, TILE), scnt[i * per_chunk], jnp.int32)
        for q in range(1, per_chunk):
            row = jnp.where(lane1 >= q * slots, scnt[i * per_chunk + q], row)
        cntm[i:i + 1, :] = row
    sidx[0:nb, :] = jnp.transpose(sidx_t[...])
    idx = jnp.concatenate(
        [sidx[pl.ds(q, chunks, stride=per_chunk), :] for q in range(per_chunk)], axis=1
    )
    slot_of = lax.rem(iota((chunks, TILE), 1), slots)
    idxm[0:chunks, :] = jnp.where(slot_of < cntm[0:chunks, :], idx, -1).astype(F32)
    loads[3].wait()
    idxm[chunks:chunks + 1, :] = hub[...].astype(F32)
    loads[2].wait()

    lane_rows = iota((TILE, rows), 1).astype(F32)

    def gather(row):
        column = jnp.transpose(jnp.broadcast_to(row, (TILE, TILE)))
        wide = jnp.concatenate([column] * row_tiles, axis=1)
        onehot = jnp.where(wide == lane_rows, 1.0, 0.0).astype(BF16)
        return dot(onehot, feat[...]).astype(BF16)

    turns_back = range(per_chunk - 1, -1, -1)
    few = nz // per_chunk if nz >= per_chunk else 1
    firsts = [(m, min(m + few, nz)) for m in range(0, nz, few)]
    rounds = [[(m, 1, q) for q in turns_back for m in range(*part_of)] for part_of in firsts]
    rounds += [[(m, 0, q) for m in range(nz)] for q in turns_back]

    def to_z(m):
        step = (m + 1) // 2
        return lax.rem(z + jnp.where(lax.rem(m, 2) == 1, nz // 2 - step, nz - nz // 2 + step), nz)

    def to_half(e):
        return lax.rem(half + e, halves)

    mine = pl.ds(pl.multiple_of(((half * nz + z) * per_chunk + lane_dev) * slots, slots), slots)

    far_first = [(nz // 2 + (m + 1) // 2 * (-1) ** m) % nz for m in range(nz)]
    chunk_to = {(m, e): lax.rem(z + far_first[m], nz) * halves + to_half(e) for m in range(nz) for e in range(halves)}

    def exchange(buffer, landing, ssem, rsem, some):
        for m, e, q in some:
            piece = lax.rem(lane_dev + q, per_chunk)
            source = buffer.at[e, m, pl.ds(pl.multiple_of(piece * slots, slots), slots)]
            if (m, e, q) == (nz - 1, 0, 0):
                pltpu.make_async_copy(source, landing.at[mine], rsem.at[0]).start()
            else:
                pltpu.make_async_remote_copy(
                    src_ref=source, dst_ref=landing.at[mine], send_sem=ssem, recv_sem=rsem.at[e],
                    device_id=(chunk_to[m, e] * per_chunk + piece, g), device_id_type=MESH,
                ).start()

    def landed(landing, rsem, e):
        some = landing.at[pl.ds(0, span)]
        pltpu.make_async_copy(some, some, rsem.at[e]).wait()
        return pl.ds(pl.multiple_of(to_half(e) * span, TILE), span)

    def gather_some(e, lo, hi):
        def at(m, _):
            sendbuf[e, m] = gather(idxm[pl.ds(to_z(m) * halves + to_half(e), 1), :])
            return 0

        lax.fori_loop(lo, hi, at, 0)

    hubsend[...] = gather(idxm[chunks:chunks + 1, :])
    hubs[g] = hubsend[...]
    early = 4
    for part_of in firsts[:early]:
        gather_some(1, *part_of)
    pl.semaphore_wait(barrier, greeted)
    for k in range(1, ng):
        pltpu.make_async_remote_copy(
            src_ref=hubsend, dst_ref=hubs.at[g], send_sem=sh1, recv_sem=rh1,
            device_id=(b, lax.rem(g + k, ng)), device_id_type=MESH,
        ).start()

    def turns(produce, ready, buffer, landing, ssem, rsem, between):
        for i, some in enumerate(rounds):
            if i < len(firsts):
                if i >= ready:
                    produce(1, *firsts[i])
                exchange(buffer, landing, ssem, rsem, some)
                produce(0, *firsts[i])
            else:
                exchange(buffer, landing, ssem, rsem, some)
            between(i)

    turns(gather_some, early, sendbuf, incoming, s1, r1, lambda i: None)

    loads[4].wait()
    loads[5].wait()
    cells = row_tiles * src_tiles
    pad = jnp.full((1, TILE - tile_count), cells + 4, jnp.int32)
    key = jnp.concatenate([trow[...] * src_tiles + tcol[...], pad], axis=1) if tile_count < TILE else trow[...] * src_tiles + tcol[...]
    full = (TILE, TILE)
    lane = iota(full, 1)
    sub = iota(full, 0)

    def count(mask, values=1):
        return jnp.sum(jnp.where(mask, values, 0), axis=0, keepdims=True)

    key_l = jnp.broadcast_to(key, full)
    key_s = jnp.transpose(key_l)
    before = jnp.logical_or(key_s < key_l, jnp.logical_and(key_s == key_l, sub < lane))
    rank_s = jnp.transpose(jnp.broadcast_to(count(before), full))
    sorted_key = count(rank_s == lane, key_s)
    former_key = count(rank_s == lane - 1, key_s)
    first = jnp.where(jnp.logical_or(sorted_key != former_key, lane[0:1] == 0), 1, 0)
    upto = count(key_s <= lane)
    last = jnp.where(count(key_s == lane) > 0, upto - 1, tile_count)
    info[0:1, :] = jnp.clip(count(rank_s == lane, sub), 0, tile_count - 1)
    info[1:2, :] = first
    info[2:3, :] = jnp.clip(last, 0, tile_count)
    info[3:8, :] = jnp.zeros((5, TILE), jnp.int32)
    to_scalars = pltpu.make_async_copy(info, info_s, loc_sem)
    to_scalars.start()
    to_scalars.wait()

    loads[6].wait()
    run[tile_count] = jnp.zeros(full, BF16)
    runT[tile_count] = jnp.zeros(full, BF16)

    def add_tile(k, total):
        value = tiles[jnp.clip(info_s[0, k], 0, tile_count - 1)].astype(F32)
        total = jnp.where(info_s[1, k] == 1, value, total + value)
        run[k] = total.astype(BF16)
        runT[k] = jnp.transpose(total).astype(BF16)
        return total

    lax.fori_loop(0, tile_count, add_tile, jnp.zeros(full, F32))

    def place(c, _):
        bound = c - row_tiles
        moved = row_tiles + lax.rem(bound, halves) * nz + bound // halves
        within = jnp.logical_and(bound >= 0, bound < chunks)
        at = pl.ds(pl.multiple_of(jnp.where(within, moved, c) * TILE, TILE), TILE)
        for r in range(row_tiles):
            cell = jnp.clip(info_s[2, r * src_tiles + c], 0, tile_count)
            A[r * TILE:(r + 1) * TILE, at] = run[cell]
            AT[c, :, r * TILE:(r + 1) * TILE] = runT[cell]
        return 0

    lax.fori_loop(0, src_tiles, place, 0)

    sub_rows = iota((rows, TILE), 0).astype(F32)

    def columns(i, _):
        row = idxm[pl.ds(i, 1), :]
        place_at = lax.rem(i, halves) * nz + i // halves
        ohT[:, pl.ds(pl.multiple_of(place_at * TILE, TILE), TILE)] = jnp.where(sub_rows == row, 1.0, 0.0).astype(BF16)
        return 0

    lax.fori_loop(0, chunks, columns, 0)
    ohhubT[...] = jnp.where(sub_rows == idxm[chunks:chunks + 1, :], 1.0, 0.0).astype(BF16)

    lo, hi = rows, rows + chunks * TILE
    pltpu.make_async_copy(hubs.at[pl.ds(0, ng - 1)], hubs.at[pl.ds(0, ng - 1)], rh1).wait()
    agg[...] = dot(A[:, 0:lo], feat[...]) + dot(A[:, hi:], hubs[...].reshape(ng * TILE, TILE))
    for i in range(7, 9):
        loads[i].wait()
    wt[...] = jnp.transpose(w[...].astype(F32)).astype(BF16)

    for e in reversed(range(halves)):
        at = landed(incoming, r1, e)
        columns_at = pl.ds(pl.multiple_of(lo + to_half(e) * span, TILE), span)
        agg[...] = agg[...] + dot(A[:, columns_at], incoming[at, :])
    for r in range(row_tiles):
        at = slice(r * TILE, (r + 1) * TILE)
        summed = agg[at, :].astype(BF16)
        aggb[at, :] = summed
        preact = dot(summed, w[...])
        logistic = 1.0 / (1.0 + jnp.exp(-preact))
        act[at, :] = (preact * logistic).astype(BF16)
        grad = (cot[at, :].astype(F32) * (logistic * (1.0 + preact * (1.0 - logistic)))).astype(BF16)
        pg[at, :] = grad
        gb[at, :] = dot(grad, wt[...]).astype(BF16)

    part[...] = dot_t(aggb[...], pg[...])
    members, blocks = q3.shape[0], q3.shape[1]
    wide = w.shape[1] // TILE
    for n in range(members * blocks):
        q3[n // blocks, n % blocks] = part[(n // wide) * 8:(n // wide) * 8 + 8, (n % wide) * TILE:(n % wide + 1) * TILE]

    def over_plane(source, target, i):
        def send(k, _):
            to = lax.rem(u + k, members)
            pltpu.make_async_remote_copy(
                src_ref=source(to), dst_ref=target(k), send_sem=ar_s.at[i], recv_sem=ar_r.at[i],
                device_id=(z * inner + lax.rem(to, inner), to // inner), device_id_type=MESH,
            ).start()
            return 0

        lax.fori_loop(1, members, send, 0)

    over_plane(lambda to: q3.at[to], lambda k: xbuf.at[members - 1 - k], 0)

    def over_z():
        pltpu.make_async_copy(xbuf, xbuf, ar_r.at[0]).wait()
        summed = q3[u]
        for k in range(members - 1):
            summed = summed + xbuf[k]
        zown[...] = summed
        zbuf[z] = summed

        def send_z(k, _):
            pltpu.make_async_remote_copy(
                src_ref=zown, dst_ref=zbuf.at[z], send_sem=ar_s.at[1], recv_sem=ar_r.at[1],
                device_id=(lax.rem(z + k, nz) * inner + ii, g), device_id_type=MESH,
            ).start()
            return 0

        lax.fori_loop(1, nz, send_z, 0)

    def back_plane():
        others = zbuf.at[pl.ds(0, nz - 1)]
        pltpu.make_async_copy(others, others, ar_r.at[1]).wait()
        total = zbuf[0]
        for k in range(1, nz):
            total = total + zbuf[k]
        f3[u] = total
        over_plane(lambda to: f3.at[u], lambda k: f3.at[u], 2)

    def finish_weight():
        others = f3.at[pl.ds(0, members - 1)]
        pltpu.make_async_copy(others, others, ar_r.at[2]).wait()
        for n in range(members * blocks):
            wg[(n // wide) * 8:(n // wide) * 8 + 8, (n % wide) * TILE:(n % wide + 1) * TILE] = f3[n // blocks, n % blocks]

    def back_some(e, lo, hi):
        def at(m, _):
            retbuf[e, m] = dot(AT[row_tiles + to_z(m) * halves + to_half(e)], gb[...]).astype(BF16)
            return 0

        lax.fori_loop(lo, hi, at, 0)

    def back_hubs():
        for k in range(ng):
            hubret_send[k] = dot(AT[row_tiles + chunks + k], gb[...]).astype(BF16)
        for k in range(1, ng):
            to = lax.rem(g + k, ng)
            pltpu.make_async_remote_copy(
                src_ref=hubret_send.at[to], dst_ref=hubret.at[ng - 1 - k], send_sem=sh2, recv_sem=rh2,
                device_id=(b, to), device_id_type=MESH,
            ).start()

    plan = {1: back_hubs, 3: over_z, 6: back_plane}
    turns(back_some, 0, retbuf, ret, s2, r2, lambda i: plan.get(i, lambda: None)())
    for r in range(row_tiles):
        fg[r * TILE:(r + 1) * TILE, :] = dot(AT[r], gb[...])

    pltpu.make_async_copy(hubret, hubret, rh2).wait()
    hub_sum = hubret_send[g].astype(F32)
    for k in range(ng - 1):
        hub_sum = hub_sum + hubret[k].astype(F32)
    hub_hi = hub_sum.astype(BF16)
    hub_lo = (hub_sum - hub_hi.astype(F32)).astype(BF16)
    fg[...] = fg[...] + dot(ohhubT[...], hub_hi) + dot(ohhubT[...], hub_lo)
    for e in reversed(range(halves)):
        at = landed(ret, r2, e)
        fg[...] = fg[...] + dot(ohT[:, at], ret[at, :])
    finish_weight()

    flat = pl.ds(0, (nb - 1) * slots)
    drop = ret.at[flat]
    pltpu.make_async_copy(drop, drop, s1).wait()
    pltpu.make_async_copy(drop, drop, s2).wait()
    pltpu.make_async_copy(hubret, hubret, sh1).wait()
    pltpu.make_async_copy(hubret, hubret, sh2).wait()
    others = zbuf.at[pl.ds(0, nz - 1)]
    pltpu.make_async_copy(xbuf, xbuf, ar_s.at[0]).wait()
    pltpu.make_async_copy(others, others, ar_s.at[1]).wait()
    pltpu.make_async_copy(xbuf, xbuf, ar_s.at[2]).wait()


def hand_out(a, b, c, a_out, b_out, c_out, sems):
    copies = [
        pltpu.make_async_copy(source, target, sems.at[i])
        for i, (source, target) in enumerate([(a, a_out), (b, b_out), (c, c_out)])
    ]
    for copy in copies:
        copy.start()
    for copy in copies:
        copy.wait()


def body(nb, ng, features, weight, cotangent, tiles, tile_row, tile_col, hub_index, send_index, send_count):
    rows, fin = features.shape
    fout = weight.shape[1]
    tile_count = tiles.shape[0]
    slots = send_index.shape[1]
    inner = 8
    nz = nb // inner
    chunks = nb * slots // TILE
    row_tiles = rows // TILE
    src_tiles = row_tiles + chunks + ng
    idx_rows = (chunks + 8) // 8 * 8
    members = ng * inner
    blocks = (fin // 8) * (fout // TILE) // members
    vm = pltpu.VMEM
    dma = pltpu.SemaphoreType.DMA
    scratch = [
        vm((rows, fin), BF16), vm((fin, fout), BF16), vm((fout, fin), BF16), vm((rows, fout), BF16),
        vm((tile_count, TILE, TILE), BF16), vm((1, tile_count), jnp.int32), vm((1, tile_count), jnp.int32),
        vm((1, TILE), jnp.int32), vm((slots, nb), jnp.int32), pltpu.SMEM((nb,), jnp.int32),
        vm((nb + 8, slots), jnp.int32),
        vm((idx_rows, TILE), jnp.int32), vm((idx_rows, TILE), F32), vm((2, nz, TILE, fin), BF16),
        vm((nb * slots, fin), BF16), vm((ng, TILE, fin), BF16), vm((TILE, fin), BF16),
        vm((rows, chunks * TILE), BF16), vm((rows, TILE), BF16),
        vm((8, TILE), jnp.int32), pltpu.SMEM((8, TILE), jnp.int32),
        vm((tile_count + 1, TILE, TILE), BF16), vm((tile_count + 1, TILE, TILE), BF16),
        vm((rows, src_tiles * TILE), BF16), vm((src_tiles, TILE, rows), BF16),
        vm((rows, fin), F32), vm((rows, fin), BF16), vm((rows, fout), BF16), vm((rows, fin), BF16),
        vm((2, nz, TILE, fin), BF16), vm((nb * slots, fin), BF16),
        vm((ng, TILE, fin), BF16), vm((ng - 1, TILE, fin), BF16),
        vm((fin, fout), F32), vm((members, blocks, 8, TILE), F32), vm((members - 1, blocks, 8, TILE), F32),
        vm((nz, blocks, 8, TILE), F32), vm((blocks, 8, TILE), F32), vm((members, blocks, 8, TILE), F32),
        dma((9,)), dma, dma((2,)), dma, dma, dma, dma((2,)), dma, dma, dma((3,)), dma((3,)), dma,
    ]
    flops = 2 * (2 * rows * src_tiles * TILE * fin + 2 * rows * chunks * TILE * fin + 3 * rows * fin * fout)
    results = pl.pallas_call(
        functools.partial(kernel, nb, ng, inner),
        out_shape=[vm((rows, fout), BF16), vm((fin, fout), F32), vm((rows, fin), F32)],
        in_specs=[pl.BlockSpec(memory_space=pl.ANY)] * 9,
        out_specs=[pl.BlockSpec(memory_space=pltpu.VMEM)] * 3,
        scratch_shapes=scratch,
        compiler_params=pltpu.CompilerParams(
            collective_id=0, has_side_effects=True, vmem_limit_bytes=56 * 1024 * 1024
        ),
        cost_estimate=pl.CostEstimate(flops=flops, bytes_accessed=4 * 1024 * 1024, transcendentals=rows * fout),
    )(
        features, weight, cotangent, tiles, tile_row.reshape(1, tile_count),
        tile_col.reshape(1, tile_count), hub_index.reshape(1, TILE), send_index.T, send_count,
    )
    return pl.pallas_call(
        hand_out,
        out_shape=[jax.ShapeDtypeStruct(result.shape, result.dtype) for result in results],
        in_specs=[pl.BlockSpec(memory_space=pl.ANY)] * 3,
        out_specs=[pl.BlockSpec(memory_space=pl.ANY)] * 3,
        scratch_shapes=[dma((3,))],
        compiler_params=pltpu.CompilerParams(vmem_limit_bytes=1024 * 1024),
    )(*results)


def solution(mesh):
    both = ("blk", "grp")
    return jax.shard_map(
        functools.partial(body, mesh.shape["blk"], mesh.shape["grp"]),
        mesh=mesh,
        in_specs=(
            P(both, None), P(), P(both, None), P(both, None, None), P(both), P(both), P(both),
            P(both, None), P(both),
        ),
        out_specs=(P(both, None), P(), P(both, None)),
        check_vma=False,
    )
```

```python
import functools

import jax
import jax.numpy as jnp
from jax import lax
from jax.experimental import pallas as pl
from jax.experimental.pallas import tpu as pltpu
from jax.sharding import PartitionSpec as P

TILE = 128
MESH = pl.DeviceIdType.MESH
BF16 = jnp.bfloat16
F32 = jnp.float32


def dot(left, right):
    return lax.dot_general(left, right, (((1,), (0,)), ((), ())), preferred_element_type=F32)


def dot_t(left, right):
    return lax.dot_general(left, right, (((0,), (0,)), ((), ())), preferred_element_type=F32)


def iota(shape, axis):
    return lax.broadcasted_iota(jnp.int32, shape, axis)


def kernel(
    nb, ng, inner,
    feat_h, w_h, cot_h, tiles_h, trow_h, tcol_h, hub_h, sidx_h, scnt_h,
    act, wg, fg,
    feat, w, wt, cot, tiles, trow, tcol, hub, sidx_t, scnt, sidx,
    cntm, idxm, sendbuf, incoming, hubs, hubsend, ohT, ohhubT,
    info, info_s, run, runT, A, AT, agg, aggb, pg, gb, retbuf, ret, hubret_send, hubret,
    part, q3, xbuf, zbuf, zown, f3,
    in_sems, s1, r1, sh1, rh1, s2, r2, sh2, rh2, ar_s, ar_r, loc_sem,
):
    rows = feat.shape[0]
    row_tiles = rows // TILE
    slots = sidx_t.shape[0]
    per_chunk = TILE // slots
    chunks = nb // per_chunk
    tile_count = tiles.shape[0]
    nz = nb // inner
    halves = inner // per_chunk
    src_tiles = row_tiles + chunks + ng
    span = nz * TILE
    b = lax.axis_index("blk")
    g = lax.axis_index("grp")
    z = b // inner
    ii = lax.rem(b, inner)
    half = ii // per_chunk
    lane_dev = lax.rem(b, per_chunk)
    u = g * inner + ii

    ins = [
        (sidx_h, sidx_t), (scnt_h, scnt), (feat_h, feat), (hub_h, hub), (trow_h, trow),
        (tcol_h, tcol), (tiles_h, tiles), (w_h, w), (cot_h, cot),
    ]
    loads = [pltpu.make_async_copy(h, v, in_sems.at[i]) for i, (h, v) in enumerate(ins)]
    for load in loads[:4]:
        load.start()

    barrier = pltpu.get_barrier_semaphore()

    def greet_z(k, _):
        to = lax.rem(z * inner + k, nb)
        pl.semaphore_signal(barrier, inc=1, device_id=(to, g), device_id_type=MESH)
        return 0

    def greet_grp(k, _):
        to = lax.rem(u + k, ng * inner)
        pl.semaphore_signal(barrier, inc=1, device_id=(z * inner + lax.rem(to, inner), to // inner), device_id_type=MESH)
        return 0

    greeted = nb - inner + ng * inner - 1
    lax.fori_loop(inner, nb, greet_z, 0)
    lax.fori_loop(1, ng * inner, greet_grp, 0)
    for load in loads[4:]:
        load.start()

    loads[0].wait()
    loads[1].wait()
    lane1 = iota((1, TILE), 1)
    for i in range(chunks):
        row = jnp.full((1, TILE), scnt[i * per_chunk], jnp.int32)
        for q in range(1, per_chunk):
            row = jnp.where(lane1 >= q * slots, scnt[i * per_chunk + q], row)
        cntm[i:i + 1, :] = row
    sidx[0:nb, :] = jnp.transpose(sidx_t[...])
    idx = jnp.concatenate(
        [sidx[pl.ds(q, chunks, stride=per_chunk), :] for q in range(per_chunk)], axis=1
    )
    slot_of = lax.rem(iota((chunks, TILE), 1), slots)
    idxm[0:chunks, :] = jnp.where(slot_of < cntm[0:chunks, :], idx, -1).astype(F32)
    loads[3].wait()
    idxm[chunks:chunks + 1, :] = hub[...].astype(F32)
    loads[2].wait()

    lane_rows = iota((TILE, rows), 1).astype(F32)

    def gather(row):
        column = jnp.transpose(jnp.broadcast_to(row, (TILE, TILE)))
        wide = jnp.concatenate([column] * row_tiles, axis=1)
        onehot = jnp.where(wide == lane_rows, 1.0, 0.0).astype(BF16)
        return dot(onehot, feat[...]).astype(BF16)

    turns_back = range(per_chunk - 1, -1, -1)
    few = nz // per_chunk if nz >= per_chunk else 1
    firsts = [(m, min(m + few, nz)) for m in range(0, nz, few)]
    rounds = [[(m, 1, q) for q in turns_back for m in range(*part_of)] for part_of in firsts]
    rounds += [[(m, 0, q) for m in range(nz)] for q in turns_back]

    def to_z(m):
        step = (m + 1) // 2
        return lax.rem(z + jnp.where(lax.rem(m, 2) == 1, nz // 2 - step, nz - nz // 2 + step), nz)

    def to_half(e):
        return lax.rem(half + e, halves)

    mine = pl.ds(pl.multiple_of(((half * nz + z) * per_chunk + lane_dev) * slots, slots), slots)

    far_first = [(nz // 2 + (m + 1) // 2 * (-1) ** m) % nz for m in range(nz)]
    chunk_to = {(m, e): lax.rem(z + far_first[m], nz) * halves + to_half(e) for m in range(nz) for e in range(halves)}

    def exchange(buffer, landing, ssem, rsem, some):
        for m, e, q in some:
            piece = lax.rem(lane_dev + q, per_chunk)
            source = buffer.at[e, m, pl.ds(pl.multiple_of(piece * slots, slots), slots)]
            if (m, e, q) == (nz - 1, 0, 0):
                pltpu.make_async_copy(source, landing.at[mine], rsem.at[0]).start()
            else:
                pltpu.make_async_remote_copy(
                    src_ref=source, dst_ref=landing.at[mine], send_sem=ssem, recv_sem=rsem.at[e],
                    device_id=(chunk_to[m, e] * per_chunk + piece, g), device_id_type=MESH,
                ).start()

    def landed(landing, rsem, e):
        some = landing.at[pl.ds(0, span)]
        pltpu.make_async_copy(some, some, rsem.at[e]).wait()
        return pl.ds(pl.multiple_of(to_half(e) * span, TILE), span)

    def gather_some(e, lo, hi):
        def at(m, _):
            sendbuf[e, m] = gather(idxm[pl.ds(to_z(m) * halves + to_half(e), 1), :])
            return 0

        lax.fori_loop(lo, hi, at, 0)

    hubsend[...] = gather(idxm[chunks:chunks + 1, :])
    hubs[g] = hubsend[...]
    early = 4
    for part_of in firsts[:early]:
        gather_some(1, *part_of)
    pl.semaphore_wait(barrier, greeted)
    for k in range(1, ng):
        pltpu.make_async_remote_copy(
            src_ref=hubsend, dst_ref=hubs.at[g], send_sem=sh1, recv_sem=rh1,
            device_id=(b, lax.rem(g + k, ng)), device_id_type=MESH,
        ).start()

    def turns(produce, ready, buffer, landing, ssem, rsem, between):
        for i, some in enumerate(rounds):
            if i < len(firsts):
                if i >= ready:
                    produce(1, *firsts[i])
                exchange(buffer, landing, ssem, rsem, some)
                produce(0, *firsts[i])
            else:
                exchange(buffer, landing, ssem, rsem, some)
            between(i)

    turns(gather_some, early, sendbuf, incoming, s1, r1, lambda i: None)

    loads[4].wait()
    loads[5].wait()
    cells = row_tiles * src_tiles
    pad = jnp.full((1, TILE - tile_count), cells + 4, jnp.int32)
    key = jnp.concatenate([trow[...] * src_tiles + tcol[...], pad], axis=1) if tile_count < TILE else trow[...] * src_tiles + tcol[...]
    full = (TILE, TILE)
    lane = iota(full, 1)
    sub = iota(full, 0)

    def count(mask, values=1):
        return jnp.sum(jnp.where(mask, values, 0), axis=0, keepdims=True)

    key_l = jnp.broadcast_to(key, full)
    key_s = jnp.transpose(key_l)
    before = jnp.logical_or(key_s < key_l, jnp.logical_and(key_s == key_l, sub < lane))
    rank_s = jnp.transpose(jnp.broadcast_to(count(before), full))
    sorted_key = count(rank_s == lane, key_s)
    former_key = count(rank_s == lane - 1, key_s)
    first = jnp.where(jnp.logical_or(sorted_key != former_key, lane[0:1] == 0), 1, 0)
    upto = count(key_s <= lane)
    last = jnp.where(count(key_s == lane) > 0, upto - 1, tile_count)
    info[0:1, :] = jnp.clip(count(rank_s == lane, sub), 0, tile_count - 1)
    info[1:2, :] = first
    info[2:3, :] = jnp.clip(last, 0, tile_count)
    info[3:8, :] = jnp.zeros((5, TILE), jnp.int32)
    to_scalars = pltpu.make_async_copy(info, info_s, loc_sem)
    to_scalars.start()
    to_scalars.wait()

    loads[6].wait()
    run[tile_count] = jnp.zeros(full, BF16)
    runT[tile_count] = jnp.zeros(full, BF16)

    def add_tile(k, total):
        value = tiles[jnp.clip(info_s[0, k], 0, tile_count - 1)].astype(F32)
        total = jnp.where(info_s[1, k] == 1, value, total + value)
        run[k] = total.astype(BF16)
        runT[k] = jnp.transpose(total).astype(BF16)
        return total

    lax.fori_loop(0, tile_count, add_tile, jnp.zeros(full, F32))

    def place(c, _):
        bound = c - row_tiles
        moved = row_tiles + lax.rem(bound, halves) * nz + bound // halves
        within = jnp.logical_and(bound >= 0, bound < chunks)
        at = pl.ds(pl.multiple_of(jnp.where(within, moved, c) * TILE, TILE), TILE)
        for r in range(row_tiles):
            cell = jnp.clip(info_s[2, r * src_tiles + c], 0, tile_count)
            A[r * TILE:(r + 1) * TILE, at] = run[cell]
            AT[c, :, r * TILE:(r + 1) * TILE] = runT[cell]
        return 0

    lax.fori_loop(0, src_tiles, place, 0)

    sub_rows = iota((rows, TILE), 0).astype(F32)

    def columns(i, _):
        row = idxm[pl.ds(i, 1), :]
        place_at = lax.rem(i, halves) * nz + i // halves
        ohT[:, pl.ds(pl.multiple_of(place_at * TILE, TILE), TILE)] = jnp.where(sub_rows == row, 1.0, 0.0).astype(BF16)
        return 0

    lax.fori_loop(0, chunks, columns, 0)
    ohhubT[...] = jnp.where(sub_rows == idxm[chunks:chunks + 1, :], 1.0, 0.0).astype(BF16)

    lo, hi = rows, rows + chunks * TILE
    pltpu.make_async_copy(hubs.at[pl.ds(0, ng - 1)], hubs.at[pl.ds(0, ng - 1)], rh1).wait()
    agg[...] = dot(A[:, 0:lo], feat[...]) + dot(A[:, hi:], hubs[...].reshape(ng * TILE, TILE))
    for i in range(7, 9):
        loads[i].wait()
    wt[...] = jnp.transpose(w[...].astype(F32)).astype(BF16)

    for e in reversed(range(halves)):
        at = landed(incoming, r1, e)
        columns_at = pl.ds(pl.multiple_of(lo + to_half(e) * span, TILE), span)
        agg[...] = agg[...] + dot(A[:, columns_at], incoming[at, :])
    for r in range(row_tiles):
        at = slice(r * TILE, (r + 1) * TILE)
        summed = agg[at, :].astype(BF16)
        aggb[at, :] = summed
        preact = dot(summed, w[...])
        logistic = 1.0 / (1.0 + jnp.exp(-preact))
        act[at, :] = (preact * logistic).astype(BF16)
        grad = (cot[at, :].astype(F32) * (logistic * (1.0 + preact * (1.0 - logistic)))).astype(BF16)
        pg[at, :] = grad
        gb[at, :] = dot(grad, wt[...]).astype(BF16)

    part[...] = dot_t(aggb[...], pg[...])
    members, blocks = q3.shape[0], q3.shape[1]
    wide = w.shape[1] // TILE
    for n in range(members * blocks):
        q3[n // blocks, n % blocks] = part[(n // wide) * 8:(n // wide) * 8 + 8, (n % wide) * TILE:(n % wide + 1) * TILE]

    def over_plane(source, target, i):
        def send(k, _):
            to = lax.rem(u + k, members)
            pltpu.make_async_remote_copy(
                src_ref=source(to), dst_ref=target(k), send_sem=ar_s.at[i], recv_sem=ar_r.at[i],
                device_id=(z * inner + lax.rem(to, inner), to // inner), device_id_type=MESH,
            ).start()
            return 0

        lax.fori_loop(1, members, send, 0)

    over_plane(lambda to: q3.at[to], lambda k: xbuf.at[members - 1 - k], 0)

    def over_z():
        pltpu.make_async_copy(xbuf, xbuf, ar_r.at[0]).wait()
        summed = q3[u]
        for k in range(members - 1):
            summed = summed + xbuf[k]
        zown[...] = summed
        zbuf[z] = summed

        def send_z(k, _):
            pltpu.make_async_remote_copy(
                src_ref=zown, dst_ref=zbuf.at[z], send_sem=ar_s.at[1], recv_sem=ar_r.at[1],
                device_id=(lax.rem(z + k, nz) * inner + ii, g), device_id_type=MESH,
            ).start()
            return 0

        lax.fori_loop(1, nz, send_z, 0)

    def back_plane():
        others = zbuf.at[pl.ds(0, nz - 1)]
        pltpu.make_async_copy(others, others, ar_r.at[1]).wait()
        total = zbuf[0]
        for k in range(1, nz):
            total = total + zbuf[k]
        f3[u] = total
        over_plane(lambda to: f3.at[u], lambda k: f3.at[u], 2)

    def finish_weight():
        others = f3.at[pl.ds(0, members - 1)]
        pltpu.make_async_copy(others, others, ar_r.at[2]).wait()
        for n in range(members * blocks):
            wg[(n // wide) * 8:(n // wide) * 8 + 8, (n % wide) * TILE:(n % wide + 1) * TILE] = f3[n // blocks, n % blocks]

    def back_some(e, lo, hi):
        def at(m, _):
            retbuf[e, m] = dot(AT[row_tiles + to_z(m) * halves + to_half(e)], gb[...]).astype(BF16)
            return 0

        lax.fori_loop(lo, hi, at, 0)

    def back_hubs():
        for k in range(ng):
            hubret_send[k] = dot(AT[row_tiles + chunks + k], gb[...]).astype(BF16)
        for k in range(1, ng):
            to = lax.rem(g + k, ng)
            pltpu.make_async_remote_copy(
                src_ref=hubret_send.at[to], dst_ref=hubret.at[ng - 1 - k], send_sem=sh2, recv_sem=rh2,
                device_id=(b, to), device_id_type=MESH,
            ).start()

    plan = {1: back_hubs, 3: over_z, 6: back_plane}
    turns(back_some, 0, retbuf, ret, s2, r2, lambda i: plan.get(i, lambda: None)())
    for r in range(row_tiles):
        fg[r * TILE:(r + 1) * TILE, :] = dot(AT[r], gb[...])

    pltpu.make_async_copy(hubret, hubret, rh2).wait()
    hub_sum = hubret_send[g].astype(F32)
    for k in range(ng - 1):
        hub_sum = hub_sum + hubret[k].astype(F32)
    hub_hi = hub_sum.astype(BF16)
    hub_lo = (hub_sum - hub_hi.astype(F32)).astype(BF16)
    fg[...] = fg[...] + dot(ohhubT[...], hub_hi) + dot(ohhubT[...], hub_lo)
    for e in reversed(range(halves)):
        at = landed(ret, r2, e)
        fg[...] = fg[...] + dot(ohT[:, at], ret[at, :])
    finish_weight()

    flat = pl.ds(0, (nb - 1) * slots)
    drop = ret.at[flat]
    pltpu.make_async_copy(drop, drop, s1).wait()
    pltpu.make_async_copy(drop, drop, s2).wait()
    pltpu.make_async_copy(hubret, hubret, sh1).wait()
    pltpu.make_async_copy(hubret, hubret, sh2).wait()
    others = zbuf.at[pl.ds(0, nz - 1)]
    pltpu.make_async_copy(xbuf, xbuf, ar_s.at[0]).wait()
    pltpu.make_async_copy(others, others, ar_s.at[1]).wait()
    pltpu.make_async_copy(xbuf, xbuf, ar_s.at[2]).wait()


def hand_out(a, b, c, a_out, b_out, c_out, sems):
    copies = [
        pltpu.make_async_copy(source, target, sems.at[i])
        for i, (source, target) in enumerate([(a, a_out), (b, b_out), (c, c_out)])
    ]
    for copy in copies:
        copy.start()
    for copy in copies:
        copy.wait()


def body(nb, ng, features, weight, cotangent, tiles, tile_row, tile_col, hub_index, send_index, send_count):
    rows, fin = features.shape
    fout = weight.shape[1]
    tile_count = tiles.shape[0]
    slots = send_index.shape[1]
    inner = 8
    nz = nb // inner
    chunks = nb * slots // TILE
    row_tiles = rows // TILE
    src_tiles = row_tiles + chunks + ng
    idx_rows = (chunks + 8) // 8 * 8
    members = ng * inner
    blocks = (fin // 8) * (fout // TILE) // members
    vm = pltpu.VMEM
    dma = pltpu.SemaphoreType.DMA
    scratch = [
        vm((rows, fin), BF16), vm((fin, fout), BF16), vm((fout, fin), BF16), vm((rows, fout), BF16),
        vm((tile_count, TILE, TILE), BF16), vm((1, tile_count), jnp.int32), vm((1, tile_count), jnp.int32),
        vm((1, TILE), jnp.int32), vm((slots, nb), jnp.int32), pltpu.SMEM((nb,), jnp.int32),
        vm((nb + 8, slots), jnp.int32),
        vm((idx_rows, TILE), jnp.int32), vm((idx_rows, TILE), F32), vm((2, nz, TILE, fin), BF16),
        vm((nb * slots, fin), BF16), vm((ng, TILE, fin), BF16), vm((TILE, fin), BF16),
        vm((rows, chunks * TILE), BF16), vm((rows, TILE), BF16),
        vm((8, TILE), jnp.int32), pltpu.SMEM((8, TILE), jnp.int32),
        vm((tile_count + 1, TILE, TILE), BF16), vm((tile_count + 1, TILE, TILE), BF16),
        vm((rows, src_tiles * TILE), BF16), vm((src_tiles, TILE, rows), BF16),
        vm((rows, fin), F32), vm((rows, fin), BF16), vm((rows, fout), BF16), vm((rows, fin), BF16),
        vm((2, nz, TILE, fin), BF16), vm((nb * slots, fin), BF16),
        vm((ng, TILE, fin), BF16), vm((ng - 1, TILE, fin), BF16),
        vm((fin, fout), F32), vm((members, blocks, 8, TILE), F32), vm((members - 1, blocks, 8, TILE), F32),
        vm((nz, blocks, 8, TILE), F32), vm((blocks, 8, TILE), F32), vm((members, blocks, 8, TILE), F32),
        dma((9,)), dma, dma((2,)), dma, dma, dma, dma((2,)), dma, dma, dma((3,)), dma((3,)), dma,
    ]
    flops = 2 * (2 * rows * src_tiles * TILE * fin + 2 * rows * chunks * TILE * fin + 3 * rows * fin * fout)
    results = pl.pallas_call(
        functools.partial(kernel, nb, ng, inner),
        out_shape=[vm((rows, fout), BF16), vm((fin, fout), F32), vm((rows, fin), F32)],
        in_specs=[pl.BlockSpec(memory_space=pl.ANY)] * 9,
        out_specs=[pl.BlockSpec(memory_space=pltpu.VMEM)] * 3,
        scratch_shapes=scratch,
        compiler_params=pltpu.CompilerParams(
            collective_id=0, has_side_effects=True, vmem_limit_bytes=56 * 1024 * 1024
        ),
        cost_estimate=pl.CostEstimate(flops=flops, bytes_accessed=4 * 1024 * 1024, transcendentals=rows * fout),
    )(
        features, weight, cotangent, tiles, tile_row.reshape(1, tile_count),
        tile_col.reshape(1, tile_count), hub_index.reshape(1, TILE), send_index.T, send_count,
    )
    return pl.pallas_call(
        hand_out,
        out_shape=[jax.ShapeDtypeStruct(result.shape, result.dtype) for result in results],
        in_specs=[pl.BlockSpec(memory_space=pl.ANY)] * 3,
        out_specs=[pl.BlockSpec(memory_space=pl.ANY)] * 3,
        scratch_shapes=[dma((3,))],
        compiler_params=pltpu.CompilerParams(vmem_limit_bytes=1024 * 1024),
    )(*results)


def solution(mesh):
    both = ("blk", "grp")
    return jax.shard_map(
        functools.partial(body, mesh.shape["blk"], mesh.shape["grp"]),
        mesh=mesh,
        in_specs=(
            P(both, None), P(), P(both, None), P(both, None, None), P(both), P(both), P(both),
            P(both, None), P(both),
        ),
        out_specs=(P(both, None), P(), P(both, None)),
        check_vma=False,
    )
```
